256 devices in a mesh: wide: 64 (over y_lo, z, x), narrow: 4 (over y_hi, core).
Axes of the slice: x: 4, y: 4 (y_hi: 2, y_lo: 2; y = y_hi * 2 + y_lo), z: 8, core: 2. Of those that a mesh axis runs over, the one named last changes fastest.
Arguments:
- echoes: bfloat16 [2, 4096, 16384], P(None, ('wide', 'narrow')), may hold values from -6 to 6
- chirp_spectrum: float32 [2, 16384], replicated, may hold values from -4 to 4
- fm_rate: float32 [16384], replicated, may hold values from 3.5762787e-05 to 0.00014305115
- range_scale: int32 [16384], replicated, may hold values from -103 to 103
- doppler_curve: int32 [4096], replicated, may hold values from 0 to 4096
- kernels: float32 [8, 8], replicated, may hold values from -2 to 2
Outputs:
- image: bfloat16 [2, 16384, 4096], P(None, ('wide', 'narrow'))
The draws below stay inside these ranges and needn't reach their ends.
All inputs are finite; a program needn't handle non-finite values.
Results may differ from the reference program's by a relative error of at most 0.034.
Values may be sent and summed in bfloat16 or wider, within the bound.
A program may use at most 128 MiB of HBM per device.

```python
import math
import jax
import jax.numpy as jnp
from jax import lax

PULSES = 4096
BINS = 16384
SHIFT = 12
TAPS = 8
PHASES = 8


def draw_range_scale(key, part):
    key = jax.random.fold_in(key, 11)
    subkeys = jax.random.split(key, 3)
    limit_value = 8 * SHIFT + 7
    drawn = jax.random.randint(subkeys[0], (BINS,), -limit_value, limit_value + 1, dtype=jnp.int32)
    high_spot = jax.random.randint(subkeys[1], (), 0, BINS, dtype=jnp.int32)
    low_spot = (high_spot + 1 + jax.random.randint(subkeys[2], (), 0, BINS - 1, dtype=jnp.int32)) % BINS
    return drawn.at[high_spot].set(limit_value).at[low_spot].set(-limit_value)


def draw_doppler_curve(key, part):
    key = jax.random.fold_in(key, 23)
    subkeys = jax.random.split(key, 3)
    drawn = jax.random.randint(subkeys[0], (PULSES,), 0, 4097, dtype=jnp.int32)
    high_spot = jax.random.randint(subkeys[1], (), 0, PULSES, dtype=jnp.int32)
    low_spot = (high_spot + 1 + jax.random.randint(subkeys[2], (), 0, PULSES - 1, dtype=jnp.int32)) % PULSES
    return drawn.at[high_spot].set(4096).at[low_spot].set(0)


def level_of(own_key, shape, cuts, low, top_value):
    level, own = 1.0, jax.random.fold_in(own_key, 6)
    for position, blocks in cuts:
        heights = jnp.exp(jax.random.uniform(jax.random.fold_in(own, position), (blocks,), jnp.float32, low / len(cuts), top_value / len(cuts)))
        level = level * jnp.repeat(heights, shape[position] // blocks).reshape([-1 if axis == position else 1 for axis in range(len(shape))])
    return level


def noise(stream_key, dims, width, limit, cuts=(), kind=jnp.bfloat16):
    entries = jax.random.normal(stream_key, dims, jnp.float32) * width
    if len(cuts) > 0:
        entries = level_of(stream_key, dims, cuts, -0.22, 0.18) * entries
    return jnp.clip(entries, min=-limit, max=limit).astype(kind)


def setup_inputs(seed: int = 0) -> dict:
    seeds = jax.random.split(jax.random.key(seed), 7)
    echoes = noise(seeds[0], (2, PULSES, BINS), 1.0, 6.0, ((1, 256),))
    chirp_spectrum = noise(seeds[1], (2, BINS), 0.7, 4.0, (), jnp.float32)
    fm_rate = jnp.clip(jnp.exp(jax.random.uniform(seeds[2], (BINS,), jnp.float32, math.log(3.5762786865234375e-05), math.log(0.00014305115))), 3.5762786865234375e-05, 0.00014305115)
    range_scale = draw_range_scale(jax.random.fold_in(seeds[6], 71), 0)
    doppler_curve = draw_doppler_curve(jax.random.fold_in(seeds[6], 71), 0)
    kernels = noise(seeds[5], (PHASES, TAPS), TAPS ** -0.5, 2.0, (), jnp.float32)
    return dict(echoes=echoes, chirp_spectrum=chirp_spectrum, fm_rate=fm_rate, range_scale=range_scale, doppler_curve=doppler_curve, kernels=kernels)


def rounded(values):
    return lax.optimization_barrier(values.astype(jnp.bfloat16)).astype(jnp.float32)


def as_complex(parts):
    return lax.complex(parts[0].astype(jnp.float32), parts[1].astype(jnp.float32))


def as_parts(values):
    return jnp.stack([jnp.real(values), jnp.imag(values)]).astype(jnp.bfloat16)


def reference(echoes, chirp_spectrum, fm_rate, range_scale, doppler_curve, kernels):
    block_rows = min(PULSES, 256)
    block_count = PULSES // block_rows
    block_width = min(BINS, 1024)
    width_count = BINS // block_width
    margin = SHIFT + 4
    chirp_values = lax.complex(chirp_spectrum[0], chirp_spectrum[1])

    def compress(row_block):
        spectrum = jnp.fft.fft(as_complex(row_block), axis=-1, norm="ortho") * chirp_values[None, :]
        spectrum = lax.complex(rounded(jnp.real(spectrum)), rounded(jnp.imag(spectrum)))
        return as_parts(jnp.fft.ifft(spectrum, axis=-1, norm="ortho"))

    pulse_blocks = echoes.reshape(2, block_count, block_rows, BINS).transpose(1, 0, 2, 3)
    compressed = lax.map(compress, pulse_blocks).transpose(1, 0, 2, 3).reshape(2, PULSES, BINS)

    def transform(column_block):
        return as_parts(jnp.fft.fft(as_complex(column_block), axis=0, norm="ortho"))

    range_blocks = compressed.reshape(2, PULSES, width_count, block_width).transpose(2, 0, 1, 3)
    doppler = lax.map(transform, range_blocks).transpose(1, 2, 0, 3).reshape(2, PULSES, BINS)
    padded = jnp.pad(doppler, ((0, 0), (0, 0), (margin, margin)))
    row_blocks = padded.reshape(2, block_count, block_rows, BINS + 2 * margin).transpose(1, 0, 2, 3)
    curve_blocks = doppler_curve.reshape(block_count, block_rows)
    starts = jnp.arange(block_count, dtype=jnp.int32) * block_rows

    def focus(inputs):
        row_block, curve_rows, first_row = inputs
        eighths = (range_scale[None, :] * curve_rows[:, None]) // 4096
        cell_shift = eighths // 8
        phase_index = eighths - 8 * cell_shift
        anchor = jnp.arange(BINS, dtype=jnp.int32)[None, :] + cell_shift + (margin - 3)
        summed = jnp.zeros((2, block_rows, BINS), jnp.float32)
        for tap_index in range(TAPS):
            positions = jnp.broadcast_to((anchor + tap_index)[None], (2, block_rows, BINS))
            picked = jnp.take_along_axis(row_block, positions, axis=2).astype(jnp.float32)
            summed = summed + kernels[phase_index, tap_index][None] * picked
        doppler_index = first_row + jnp.arange(block_rows, dtype=jnp.int32)
        signed = (doppler_index + PULSES // 2) % PULSES - PULSES // 2
        square = (signed * signed).astype(jnp.float32)
        angles = jnp.pi * fm_rate[None, :] * square[:, None]
        cosines = jnp.cos(angles)
        sines = jnp.sin(angles)
        real_part = summed[0] * cosines - summed[1] * sines
        imag_part = summed[0] * sines + summed[1] * cosines
        return jnp.stack([real_part, imag_part]).astype(jnp.bfloat16)

    focused = lax.map(focus, (row_blocks, curve_blocks, starts)).transpose(1, 0, 2, 3).reshape(2, PULSES, BINS)

    def invert(column_block):
        values = jnp.fft.ifft(as_complex(column_block), axis=0, norm="ortho")
        return jnp.stack([jnp.real(values).T, jnp.imag(values).T]).astype(jnp.bfloat16)

    column_blocks = focused.reshape(2, PULSES, width_count, block_width).transpose(2, 0, 1, 3)
    image = lax.map(invert, column_blocks).transpose(1, 0, 2, 3).reshape(2, BINS, PULSES)
    return image
```

```python
import functools
import math

import jax
import jax.numpy as jnp
import ml_dtypes
import numpy as np
from jax import lax
from jax.experimental import pallas as pl
from jax.experimental.pallas import tpu as pltpu
from jax.sharding import PartitionSpec as P

PULSES = 4096
BINS = 16384
EDGE = 128
LOW = 32
TAPS = 8
PHASES = 8
HALO = 16
DEVICES = 256
OWN = BINS // DEVICES
ROWS = PULSES // DEVICES
AXES = ("wide", "narrow")
F32 = jnp.float32
BF16 = jnp.bfloat16


def roots(product, total):
    angles = 2.0 * np.pi / total * (product % total)
    return np.cos(angles), np.sin(angles)


def range_tables():
    count = np.arange(EDGE)
    c, s = roots(np.outer(count, count), EDGE)
    c, s = c / math.sqrt(EDGE), s / math.sqrt(EDGE)
    fwd_left = np.block([[c, s], [-s, c]])
    inv_left = np.block([[c, -s], [s, c]])
    tables = np.stack([fwd_left, fwd_left.T, inv_left.T, inv_left])
    tc, ts = roots(np.outer(count, count), BINS)
    return tables.astype(ml_dtypes.bfloat16), np.stack([tc, ts]).astype(np.float32)


def azimuth_tables():
    low = np.arange(LOW)[:, None, None]
    n = np.arange(EDGE)[None, :, None]
    j = np.arange(EDGE)[None, None, :]
    c, s = roots(n * (low + LOW * j), PULSES)
    return (np.stack([c, s], axis=1) / math.sqrt(PULSES)).astype(ml_dtypes.bfloat16)


def fft(values, sign):
    count = len(values)
    if count == 1:
        return values
    even, odd = fft(values[0::2], sign), fft(values[1::2], sign)
    half = count // 2
    out = [None] * count
    for k in range(half):
        (ar, ai), (br, bi) = even[k], odd[k]
        if k == 0:
            tr, ti = br, bi
        elif 4 * k == count:
            tr, ti = (-bi, br) if sign > 0 else (bi, -br)
        else:
            angle = 2.0 * math.pi * k / count
            c, s = math.cos(angle), sign * math.sin(angle)
            if 8 * k == count:
                tr, ti = (br - bi * (1 if sign > 0 else -1)) * c, (bi + br * (1 if sign > 0 else -1)) * c
            else:
                tr, ti = br * c - bi * s, br * s + bi * c
        out[k] = (ar + tr, ai + ti)
        out[k + half] = (ar - tr, ai - ti)
    return out


def dot(a, b):
    return jnp.dot(a, b, preferred_element_type=F32)


def range_kernel(echo_ref, chirp_ref, table_ref, twiddle_ref, send_ref, wide_ref, turned_ref):
    def spread(m, carry):
        columns = pl.ds(pl.multiple_of(m * EDGE, EDGE), EDGE)
        for part in range(2):
            block = echo_ref[part, :, columns].astype(F32)
            wide_ref[part, pl.ds(pl.multiple_of(m * ROWS, ROWS), ROWS), :] = block
        return carry

    lax.fori_loop(0, EDGE, spread, 0, unroll=8)
    tc, ts = twiddle_ref[0], twiddle_ref[1]

    def pair(i, carry):
        b = 2 * i
        signal = jnp.concatenate(
            [
                jnp.concatenate(
                    [wide_ref[part, pl.ds(b + h, EDGE, stride=ROWS), :] for h in range(2)], axis=1
                )
                for part in range(2)
            ],
            axis=0,
        ).astype(BF16)
        first = dot(table_ref[0], signal)
        rows = []
        for h in range(2):
            re, im = first[:EDGE, h * EDGE : (h + 1) * EDGE], first[EDGE:, h * EDGE : (h + 1) * EDGE]
            rows.append(jnp.concatenate([re * tc + im * ts, im * tc - re * ts], axis=1))
        spectrum = dot(jnp.concatenate(rows, axis=0).astype(BF16), table_ref[1])
        rows = []
        for h in range(2):
            re, im = spectrum[h * EDGE : (h + 1) * EDGE, :EDGE], spectrum[h * EDGE : (h + 1) * EDGE, EDGE:]
            rows.append(
                jnp.concatenate(
                    [re * chirp_ref[0] - im * chirp_ref[1], re * chirp_ref[1] + im * chirp_ref[0]], axis=1
                )
            )
        back = dot(jnp.concatenate(rows, axis=0).astype(BF16), table_ref[2])
        columns = []
        for h in range(2):
            re, im = back[h * EDGE : (h + 1) * EDGE, :EDGE], back[h * EDGE : (h + 1) * EDGE, EDGE:]
            columns.append(jnp.concatenate([re * tc - im * ts, im * tc + re * ts], axis=0))
        result = dot(table_ref[3], jnp.concatenate(columns, axis=1).astype(BF16))
        for h in range(2):
            for part in range(2):
                turned_ref[part, pl.ds(b + h, EDGE, stride=ROWS), :] = result[
                    part * EDGE : (part + 1) * EDGE, h * EDGE : (h + 1) * EDGE
                ]
        return carry

    lax.fori_loop(0, ROWS // 2, pair, 0)
    low_half = lax.broadcasted_iota(jnp.int32, (ROWS, EDGE), 1) < EDGE // 2

    def pack(u, carry):
        rows = pl.ds(pl.multiple_of(u * ROWS, ROWS), ROWS)
        re, im = turned_ref[0, rows, :], turned_ref[1, rows, :]
        send_ref[2 * u] = jnp.where(low_half, re, pltpu.roll(im, EDGE // 2, 1)).astype(BF16)
        send_ref[2 * u + 1] = jnp.where(low_half, pltpu.roll(re, EDGE // 2, 1), im).astype(BF16)
        return carry

    lax.fori_loop(0, EDGE, pack, 0, unroll=8)


def compress(echoes, chirp, tables, twiddles):
    return pl.pallas_call(
        range_kernel,
        out_shape=jax.ShapeDtypeStruct((DEVICES, ROWS, EDGE), BF16),
        scratch_shapes=[
            pltpu.VMEM((2, EDGE * ROWS, EDGE), F32),
            pltpu.VMEM((2, EDGE * ROWS, EDGE), F32),
        ],
        compiler_params=pltpu.CompilerParams(vmem_limit_bytes=40 << 20),
        name="compress",
    )(echoes, chirp, tables, twiddles)


def split_pairs(got_ref, re_ref, im_ref):
    half = EDGE // 2
    low_half = lax.broadcasted_iota(jnp.int32, (ROWS, EDGE), 1) < half

    def step(m, carry):
        for g in range(half // ROWS):
            near = got_ref[m * 8 + g].astype(F32)
            far = got_ref[m * 8 + 4 + g].astype(F32)
            rows = pl.ds(g * ROWS, ROWS)
            re_ref[m, rows, :] = jnp.where(low_half, near, pltpu.roll(far, half, 1))
            im_ref[m, rows, :] = jnp.where(low_half, pltpu.roll(near, half, 1), far)
        return carry

    lax.fori_loop(0, LOW, step, 0, unroll=2)


def low_transform(re_ref, im_ref, sign, store):
    def step(g, carry):
        rows = pl.ds(pl.multiple_of(g * 8, 8), 8)
        values = fft([(re_ref[m, rows, :], im_ref[m, rows, :]) for m in range(LOW)], sign)
        for k, (re, im) in enumerate(values):
            store(k, g, re, im)
        return carry

    lax.fori_loop(0, 8, step, 0)


def low_store(re_ref, im_ref):
    def store(k, g, re, im):
        rows = pl.ds(pl.multiple_of(g * 8, 8), 8)
        re_ref[k, rows, :] = re
        im_ref[k, rows, :] = im

    return store


def block_table(table_ref, k):
    c, s = table_ref[k, 0], table_ref[k, 1]
    return jnp.concatenate(
        [jnp.concatenate([c, -s], axis=1), jnp.concatenate([s, c], axis=1)], axis=0
    )


def doppler_kernel(got_ref, table_ref, out_ref, re_ref, im_ref, wide_ref):
    half = EDGE // 2
    split_pairs(got_ref, re_ref, im_ref)
    low_transform(re_ref, im_ref, -1, low_store(re_ref, im_ref))

    def step(k, carry):
        re, im = re_ref[k], im_ref[k]
        left = jnp.concatenate(
            [re, pltpu.roll(re, half, 1), im, pltpu.roll(im, half, 1)], axis=0
        ).astype(BF16)
        result = lax.dot_general(
            left, block_table(table_ref, k), (((0,), (0,)), ((), ())), preferred_element_type=F32
        )
        for part in range(2):
            wide_ref[part, pl.ds(k, OWN, stride=LOW), :] = result[:OWN, part * EDGE : (part + 1) * EDGE]
        return carry

    lax.fori_loop(0, LOW, step, 0)

    def narrow(r, carry):
        rows = pl.ds(pl.multiple_of(r * LOW, LOW), LOW)
        for part in range(2):
            out_ref[part, r] = wide_ref[part, rows, :].astype(BF16)
        return carry

    lax.fori_loop(0, OWN, narrow, 0, unroll=4)


def doppler_spectra(got, table):
    return pl.pallas_call(
        doppler_kernel,
        out_shape=jax.ShapeDtypeStruct((2, OWN, LOW, EDGE), BF16),
        scratch_shapes=[
            pltpu.VMEM((LOW, EDGE // 2, EDGE), F32),
            pltpu.VMEM((LOW, EDGE // 2, EDGE), F32),
            pltpu.VMEM((2, OWN * LOW, EDGE), F32),
        ],
        compiler_params=pltpu.CompilerParams(vmem_limit_bytes=40 << 20),
        name="doppler_spectra",
    )(got, table)


def turn(turns):
    x = turns - jnp.round(turns)
    y = x * x
    c = jnp.full_like(x, COS_TERMS[-1])
    for term in COS_TERMS[-2::-1]:
        c = c * y + term
    s = jnp.full_like(x, SIN_TERMS[-1])
    for term in SIN_TERMS[-2::-1]:
        s = s * y + term
    return c, s * x


def fitted_terms():
    x = np.cos(np.pi * (np.arange(400) + 0.5) / 800) * 0.5
    y = x * x
    powers = np.stack([y**i for i in range(6)], axis=1)
    c = np.linalg.lstsq(powers, np.cos(2 * np.pi * x), rcond=None)[0]
    s = np.linalg.lstsq(powers * x[:, None], np.sin(2 * np.pi * x), rcond=None)[0]
    return [float(v) for v in c], [float(v) for v in s]


COS_TERMS, SIN_TERMS = fitted_terms()


def migrate_rows(r, padded_ref, scale_ref, rate_ref, curve_ref, square_ref, taps_ref, store):
    scale = scale_ref[r]
    negative = scale < 0
    first = r + HALO - 3 - jnp.where(negative, SHIFT_LOW, 0)
    offset = jnp.where(negative, 8.0 * SHIFT_LOW, 0.0).astype(F32)
    scale = scale.astype(F32) * (1.0 / 4096.0)
    for h in range(2):
        rows = pl.ds(16 * h, 16)
        level = (jnp.floor(curve_ref[rows, :] * scale) + offset).astype(BF16)
        bits = []
        for weight in (64, 32, 16, 8, 4, 2, 1):
            bit = level >= jnp.asarray(weight, BF16)
            bits.append(bit)
            if weight > 1:
                level = jnp.where(bit, level - jnp.asarray(weight, BF16), level)
        weights = []
        for t in range(TAPS):
            level4 = [jnp.where(bits[6], taps_ref[(2 * i + 1) * TAPS + t], taps_ref[2 * i * TAPS + t]) for i in range(4)]
            level2 = [jnp.where(bits[5], level4[2 * i + 1], level4[2 * i]) for i in range(2)]
            weights.append(jnp.where(bits[4], level2[1], level2[0]))
        sums = []
        for part in range(2):
            x = [padded_ref[part, first + i, rows, :] for i in range(21)]
            x = [jnp.where(bits[0], x[i + 8], x[i]) if i < 13 else x[i] for i in range(15)]
            x = [jnp.where(bits[1], x[i + 4], x[i]) for i in range(11)]
            x = [jnp.where(bits[2], x[i + 2], x[i]) for i in range(9)]
            x = [jnp.where(bits[3], x[i + 1], x[i]) for i in range(8)]
            terms = [a * b for a, b in zip(x, weights)]
            while len(terms) > 1:
                terms = [terms[i] + terms[i + 1] for i in range(0, len(terms), 2)]
            sums.append(terms[0].astype(F32))
        c, s = turn(square_ref[rows, :] * rate_ref[r])
        store(r, h, sums[0] * c - sums[1] * s, sums[0] * s + sums[1] * c)


SHIFT_LOW = 13


def focus_kernel(
    body_ref, head_ref, tail_ref, scale_ref, rate_ref, curve_ref, square_ref, taps_ref, table_ref,
    image_ref, padded_ref, wide_ref, re_ref, im_ref,
):
    for part in range(2):
        padded_ref[part, 0:HALO] = head_ref[part]
        padded_ref[part, HALO : HALO + OWN] = body_ref[part]
        padded_ref[part, HALO + OWN : 2 * HALO + OWN] = tail_ref[part]

    def store(r, h, re, im):
        rows = pl.ds(pl.multiple_of(r * LOW + 16 * h, 16), 16)
        wide_ref[0, rows, :] = re
        wide_ref[1, rows, :] = im

    def step(r, carry):
        migrate_rows(r, padded_ref, scale_ref, rate_ref, curve_ref, square_ref, taps_ref, store)
        return carry

    lax.fori_loop(0, OWN, step, 0)

    def back(k, carry):
        left = jnp.concatenate(
            [wide_ref[part, pl.ds(k, OWN, stride=LOW), :] for part in range(2)], axis=1
        ).astype(BF16)
        result = lax.dot_general(
            left, block_table(table_ref, k), (((1,), (1,)), ((), ())), preferred_element_type=F32
        )
        re_ref[k] = result[:, :EDGE]
        im_ref[k] = result[:, EDGE:]
        return carry

    lax.fori_loop(0, LOW, back, 0)
    low_transform(re_ref, im_ref, 1, low_store(re_ref, im_ref))

    def final(h, carry):
        columns = pl.ds(pl.multiple_of(h * EDGE, EDGE), EDGE)
        image_ref[0, :, columns] = re_ref[h].astype(BF16)
        image_ref[1, :, columns] = im_ref[h].astype(BF16)
        return carry

    lax.fori_loop(0, LOW, final, 0)


def focus(body, head, tail, scales, rates, curve, square, taps, table):
    vmem, smem = pl.BlockSpec(memory_space=pltpu.VMEM), pl.BlockSpec(memory_space=pltpu.SMEM)
    return pl.pallas_call(
        focus_kernel,
        out_shape=jax.ShapeDtypeStruct((2, OWN, PULSES), BF16),
        in_specs=[vmem, vmem, vmem, smem, smem, vmem, vmem, vmem, vmem],
        out_specs=vmem,
        scratch_shapes=[
            pltpu.VMEM((2, 2 * HALO + OWN + 8, LOW, EDGE), BF16),
            pltpu.VMEM((2, OWN * LOW, EDGE), F32),
            pltpu.VMEM((LOW, OWN, EDGE), F32),
            pltpu.VMEM((LOW, OWN, EDGE), F32),
        ],
        compiler_params=pltpu.CompilerParams(vmem_limit_bytes=48 << 20),
        name="focus",
    )(body, head, tail, scales, rates, curve, square, taps, table)


def shards(echoes, chirp_spectrum, fm_rate, range_scale, doppler_curve, kernels):
    me = lax.axis_index("wide") * lax.axis_size("narrow") + lax.axis_index("narrow")
    tables, twiddles = range_tables()
    azimuth = jnp.asarray(azimuth_tables())
    chirp = chirp_spectrum.reshape(2, EDGE, EDGE).transpose(0, 2, 1)
    send = compress(echoes, chirp, jnp.asarray(tables), jnp.asarray(twiddles))
    got = lax.all_to_all(send, AXES, 0, 0, tiled=True)
    body = doppler_spectra(got, azimuth)
    head = lax.ppermute(body[:, OWN - HALO :], AXES, [(i, i + 1) for i in range(DEVICES - 1)])
    tail = lax.ppermute(body[:, :HALO], AXES, [(i + 1, i) for i in range(DEVICES - 1)])
    scales = lax.dynamic_slice_in_dim(range_scale, me * OWN, OWN)
    rates = lax.dynamic_slice_in_dim(fm_rate, me * OWN, OWN) * 0.5
    curve = doppler_curve.astype(F32).reshape(EDGE, LOW).T
    index = np.arange(PULSES)
    signed = (index + PULSES // 2) % PULSES - PULSES // 2
    square = jnp.asarray((signed * signed).astype(np.float32).reshape(EDGE, LOW).T)
    taps = jnp.broadcast_to(kernels.reshape(-1, 1, 1).astype(BF16), (PHASES * TAPS, 16, EDGE))
    return focus(body, head, tail, scales, rates, curve, square, taps, azimuth)


def solution(mesh):
    in_specs = (P(None, AXES, None), P(), P(), P(), P(), P())
    out_specs = P(None, AXES, None)
    return jax.shard_map(shards, mesh=mesh, in_specs=in_specs, out_specs=out_specs, check_vma=False)
```

```python
import functools
import math

import jax
import jax.numpy as jnp
import ml_dtypes
import numpy as np
from jax import lax
from jax.experimental import pallas as pl
from jax.experimental.pallas import tpu as pltpu
from jax.sharding import PartitionSpec as P

PULSES = 4096
BINS = 16384
EDGE = 128
LOW = 32
TAPS = 8
PHASES = 8
HALO = 16
DEVICES = 256
OWN = BINS // DEVICES
ROWS = PULSES // DEVICES
AXES = ("wide", "narrow")
F32 = jnp.float32
BF16 = jnp.bfloat16


def roots(product, total):
    angles = 2.0 * np.pi / total * (product % total)
    return np.cos(angles), np.sin(angles)


def range_tables():
    count = np.arange(EDGE)
    c, s = roots(np.outer(count, count), EDGE)
    c, s = c / math.sqrt(EDGE), s / math.sqrt(EDGE)
    fwd_left = np.block([[c, s], [-s, c]])
    inv_left = np.block([[c, -s], [s, c]])
    tables = np.stack([fwd_left, fwd_left.T, inv_left.T, inv_left])
    tc, ts = roots(np.outer(count, count), BINS)
    return tables.astype(ml_dtypes.bfloat16), np.stack([tc, ts]).astype(np.float32)


def azimuth_tables():
    low = np.arange(LOW)[:, None, None]
    n = np.arange(EDGE)[None, :, None]
    j = np.arange(EDGE)[None, None, :]
    c, s = roots(n * (low + LOW * j), PULSES)
    return (np.stack([c, s], axis=1) / math.sqrt(PULSES)).astype(ml_dtypes.bfloat16)


def fft(values, sign):
    count = len(values)
    if count == 1:
        return values
    even, odd = fft(values[0::2], sign), fft(values[1::2], sign)
    half = count // 2
    out = [None] * count
    for k in range(half):
        (ar, ai), (br, bi) = even[k], odd[k]
        if k == 0:
            tr, ti = br, bi
        elif 4 * k == count:
            tr, ti = (-bi, br) if sign > 0 else (bi, -br)
        else:
            angle = 2.0 * math.pi * k / count
            c, s = math.cos(angle), sign * math.sin(angle)
            if 8 * k == count:
                tr, ti = (br - bi * (1 if sign > 0 else -1)) * c, (bi + br * (1 if sign > 0 else -1)) * c
            else:
                tr, ti = br * c - bi * s, br * s + bi * c
        out[k] = (ar + tr, ai + ti)
        out[k + half] = (ar - tr, ai - ti)
    return out


def dot(a, b):
    return jnp.dot(a, b, preferred_element_type=F32)


MESH_IDS = pl.DeviceIdType.MESH


def place():
    wide, narrow = lax.axis_index("wide"), lax.axis_index("narrow")
    return wide % 4, (narrow // 2) * 2 + wide // 32, (wide // 4) % 8, narrow % 2


def device_at(x, y, z, core):
    return ((y % 2) * 8 + z) * 4 + x, (y // 2) * 2 + core


def signal(semaphore, x, y, z, core):
    wide, narrow = device_at(x, y, z, core)
    pl.semaphore_signal(
        semaphore, inc=1, device_id={"wide": wide, "narrow": narrow}, device_id_type=MESH_IDS
    )


def range_kernel(
    echo_ref, chirp_ref, table_ref, twiddle_ref, got_ref,
    send_ref, wide_ref, turned_ref, y_sem, z_sem, send_sem, recv_sem, own_sem,
):
    x, y, z, core = place()
    barrier = pltpu.get_barrier_semaphore()
    for i in range(1, 8):
        signal(barrier, (x + i // 2) % 4, y, z, (core + i) % 2)
    for i in range(1, 4):
        signal(barrier, x, (y + i) % 4, z, core)
    for i in range(1, 8):
        signal(barrier, x, y, (z + i) % 8, core)

    def spread(m, carry):
        columns = pl.ds(pl.multiple_of(m * EDGE, EDGE), EDGE)
        for part in range(2):
            block = echo_ref[part, :, columns].astype(F32)
            wide_ref[part, pl.ds(pl.multiple_of(m * ROWS, ROWS), ROWS), :] = block
        return carry

    lax.fori_loop(0, EDGE, spread, 0, unroll=8)

    pl.semaphore_wait(barrier, 17)
    for i in range(1, 4):
        signal(y_sem, x, (y + i) % 4, z, core)
    tc, ts = twiddle_ref[0], twiddle_ref[1]

    def pair(i, carry):
        b = 2 * i
        signals = jnp.concatenate(
            [
                jnp.concatenate(
                    [wide_ref[part, pl.ds(b + h, EDGE, stride=ROWS), :] for h in range(2)], axis=1
                )
                for part in range(2)
            ],
            axis=0,
        ).astype(BF16)
        first = dot(table_ref[0], signals)
        rows = []
        for h in range(2):
            re, im = first[:EDGE, h * EDGE : (h + 1) * EDGE], first[EDGE:, h * EDGE : (h + 1) * EDGE]
            rows.append(jnp.concatenate([re * tc + im * ts, im * tc - re * ts], axis=1))
        spectrum = dot(jnp.concatenate(rows, axis=0).astype(BF16), table_ref[1])
        rows = []
        for h in range(2):
            re, im = spectrum[h * EDGE : (h + 1) * EDGE, :EDGE], spectrum[h * EDGE : (h + 1) * EDGE, EDGE:]
            rows.append(
                jnp.concatenate(
                    [re * chirp_ref[0] - im * chirp_ref[1], re * chirp_ref[1] + im * chirp_ref[0]], axis=1
                )
            )
        back = dot(jnp.concatenate(rows, axis=0).astype(BF16), table_ref[2])
        columns = []
        for h in range(2):
            re, im = back[h * EDGE : (h + 1) * EDGE, :EDGE], back[h * EDGE : (h + 1) * EDGE, EDGE:]
            columns.append(jnp.concatenate([re * tc - im * ts, im * tc + re * ts], axis=0))
        result = dot(table_ref[3], jnp.concatenate(columns, axis=1).astype(BF16))
        for h in range(2):
            for part in range(2):
                turned_ref[part, pl.ds(b + h, EDGE, stride=ROWS), :] = result[
                    part * EDGE : (part + 1) * EDGE, h * EDGE : (h + 1) * EDGE
                ]
        return carry

    lax.fori_loop(0, ROWS // 4, pair, 0, unroll=UNROLL)
    pl.semaphore_wait(y_sem, 3)
    for i in range(1, 8):
        signal(z_sem, x, y, (z + i) % 8, core)
    lax.fori_loop(ROWS // 4, ROWS // 2, pair, 0, unroll=UNROLL)
    pl.semaphore_wait(z_sem, 7)

    low_half = lax.broadcasted_iota(jnp.int32, (ROWS, EDGE), 1) < EDGE // 2
    wide, narrow = device_at(x, y, z, core)
    me = wide * 4 + narrow

    def pack(t, carry):
        z_step = jnp.where(core == 0, t % 8, (8 - t % 8) % 8)
        x_step = (t // 8 + z_step) % 4
        y_step = (t // 32 + z_step // 2) % 4
        to_x, to_y, to_z = (x + x_step) % 4, (y + y_step) % 4, (z + z_step) % 8
        to_wide, to_narrow = device_at(to_x, to_y, to_z, 0)
        u = to_wide * 2 + to_narrow // 2
        rows = pl.ds(pl.multiple_of(u * ROWS, ROWS), ROWS)
        re, im = turned_ref[0, rows, :], turned_ref[1, rows, :]
        send_ref[2 * u] = jnp.where(low_half, re, pltpu.roll(im, EDGE // 2, 1)).astype(BF16)
        send_ref[2 * u + 1] = jnp.where(low_half, pltpu.roll(re, EDGE // 2, 1), im).astype(BF16)

        def start(to_core):
            pltpu.make_async_remote_copy(
                send_ref.at[2 * u + to_core], got_ref.at[me], send_sem, recv_sem,
                device_id={"wide": to_wide, "narrow": to_narrow + to_core}, device_id_type=MESH_IDS,
            ).start()

        @pl.when(t > 0)
        def _():
            start(0)
            start(1)

        @pl.when(t == 0)
        def _():
            start(1 - core)

        return carry

    lax.fori_loop(0, EDGE, pack, 0)
    own = pltpu.make_async_copy(send_ref.at[me], got_ref.at[me], own_sem)
    own.start()
    own.wait()
    others = pltpu.make_async_remote_copy(
        send_ref.at[pl.ds(0, DEVICES - 1)], got_ref.at[pl.ds(0, DEVICES - 1)], send_sem, recv_sem,
        device_id={"wide": wide, "narrow": (narrow + 1) % 4}, device_id_type=MESH_IDS,
    )
    others.wait_send()
    others.wait_recv()


UNROLL = 2


def compress(echoes, chirp, tables, twiddles):
    semaphores = [pltpu.SemaphoreType.REGULAR] * 2 + [pltpu.SemaphoreType.DMA] * 3
    return pl.pallas_call(
        range_kernel,
        out_shape=jax.ShapeDtypeStruct((DEVICES, ROWS, EDGE), BF16),
        in_specs=[pl.BlockSpec(memory_space=pltpu.VMEM)] * 4,
        out_specs=pl.BlockSpec(memory_space=pltpu.VMEM),
        scratch_shapes=[
            pltpu.VMEM((DEVICES, ROWS, EDGE), BF16),
            pltpu.VMEM((2, EDGE * ROWS, EDGE), F32),
            pltpu.VMEM((2, EDGE * ROWS, EDGE), F32),
        ]
        + semaphores,
        compiler_params=pltpu.CompilerParams(
            collective_id=0, has_side_effects=True, vmem_limit_bytes=40 << 20
        ),
        name="compress",
    )(echoes, chirp, tables, twiddles)


def split_pairs(got_ref, re_ref, im_ref):
    half = EDGE // 2
    low_half = lax.broadcasted_iota(jnp.int32, (ROWS, EDGE), 1) < half

    def step(m, carry):
        for g in range(half // ROWS):
            near = got_ref[m * 8 + g].astype(F32)
            far = got_ref[m * 8 + 4 + g].astype(F32)
            rows = pl.ds(g * ROWS, ROWS)
            re_ref[m, rows, :] = jnp.where(low_half, near, pltpu.roll(far, half, 1))
            im_ref[m, rows, :] = jnp.where(low_half, pltpu.roll(near, half, 1), far)
        return carry

    lax.fori_loop(0, LOW, step, 0, unroll=2)


def low_transform(re_ref, im_ref, sign, store):
    def step(g, carry):
        rows = pl.ds(pl.multiple_of(g * 8, 8), 8)
        values = fft([(re_ref[m, rows, :], im_ref[m, rows, :]) for m in range(LOW)], sign)
        for k, (re, im) in enumerate(values):
            store(k, g, re, im)
        return carry

    lax.fori_loop(0, 8, step, 0)


def low_store(re_ref, im_ref):
    def store(k, g, re, im):
        rows = pl.ds(pl.multiple_of(g * 8, 8), 8)
        re_ref[k, rows, :] = re
        im_ref[k, rows, :] = im

    return store


def block_table(table_ref, k):
    c, s = table_ref[k, 0], table_ref[k, 1]
    return jnp.concatenate(
        [jnp.concatenate([c, -s], axis=1), jnp.concatenate([s, c], axis=1)], axis=0
    )


def doppler_kernel(got_ref, table_ref, out_ref, re_ref, im_ref, wide_ref):
    half = EDGE // 2
    split_pairs(got_ref, re_ref, im_ref)
    low_transform(re_ref, im_ref, -1, low_store(re_ref, im_ref))

    def step(k, carry):
        re, im = re_ref[k], im_ref[k]
        left = jnp.concatenate(
            [re, pltpu.roll(re, half, 1), im, pltpu.roll(im, half, 1)], axis=0
        ).astype(BF16)
        result = lax.dot_general(
            left, block_table(table_ref, k), (((0,), (0,)), ((), ())), preferred_element_type=F32
        )
        for part in range(2):
            wide_ref[part, pl.ds(k, OWN, stride=LOW), :] = result[:OWN, part * EDGE : (part + 1) * EDGE]
        return carry

    lax.fori_loop(0, LOW, step, 0, unroll=4)

    def narrow(r, carry):
        rows = pl.ds(pl.multiple_of(r * LOW, LOW), LOW)
        for part in range(2):
            out_ref[part, r] = wide_ref[part, rows, :].astype(BF16)
        return carry

    lax.fori_loop(0, OWN, narrow, 0, unroll=4)


def doppler_spectra(got, table):
    return pl.pallas_call(
        doppler_kernel,
        out_shape=jax.ShapeDtypeStruct((2, OWN, LOW, EDGE), BF16),
        scratch_shapes=[
            pltpu.VMEM((LOW, EDGE // 2, EDGE), F32),
            pltpu.VMEM((LOW, EDGE // 2, EDGE), F32),
            pltpu.VMEM((2, OWN * LOW, EDGE), F32),
        ],
        compiler_params=pltpu.CompilerParams(vmem_limit_bytes=40 << 20),
        name="doppler_spectra",
    )(got, table)


def turn(turns):
    x = turns - jnp.round(turns)
    y = x * x
    c = jnp.full_like(x, COS_TERMS[-1])
    for term in COS_TERMS[-2::-1]:
        c = c * y + term
    s = jnp.full_like(x, SIN_TERMS[-1])
    for term in SIN_TERMS[-2::-1]:
        s = s * y + term
    return c, s * x


def fitted_terms():
    x = np.cos(np.pi * (np.arange(400) + 0.5) / 800) * 0.5
    y = x * x
    powers = np.stack([y**i for i in range(6)], axis=1)
    c = np.linalg.lstsq(powers, np.cos(2 * np.pi * x), rcond=None)[0]
    s = np.linalg.lstsq(powers * x[:, None], np.sin(2 * np.pi * x), rcond=None)[0]
    return [float(v) for v in c], [float(v) for v in s]


COS_TERMS, SIN_TERMS = fitted_terms()


def migrate_rows(r, padded_ref, scale_ref, rate_ref, curve_ref, square_ref, taps_ref, store):
    scale = scale_ref[r]
    negative = scale < 0
    first = r + HALO - 3 - jnp.where(negative, SHIFT_LOW, 0)
    offset = jnp.where(negative, 8.0 * SHIFT_LOW, 0.0).astype(F32)
    scale = scale.astype(F32) * (1.0 / 4096.0)
    for h in range(2):
        rows = pl.ds(16 * h, 16)
        level = (jnp.floor(curve_ref[rows, :] * scale) + offset).astype(BF16)
        bits = []
        for weight in (64, 32, 16, 8, 4, 2, 1):
            bit = level >= jnp.asarray(weight, BF16)
            bits.append(bit)
            if weight > 1:
                level = jnp.where(bit, level - jnp.asarray(weight, BF16), level)
        weights = []
        for t in range(TAPS):
            level4 = [jnp.where(bits[6], taps_ref[(2 * i + 1) * TAPS + t], taps_ref[2 * i * TAPS + t]) for i in range(4)]
            level2 = [jnp.where(bits[5], level4[2 * i + 1], level4[2 * i]) for i in range(2)]
            weights.append(jnp.where(bits[4], level2[1], level2[0]))
        sums = []
        for part in range(2):
            x = [padded_ref[part, first + i, rows, :] for i in range(21)]
            x = [jnp.where(bits[0], x[i + 8], x[i]) if i < 13 else x[i] for i in range(15)]
            x = [jnp.where(bits[1], x[i + 4], x[i]) for i in range(11)]
            x = [jnp.where(bits[2], x[i + 2], x[i]) for i in range(9)]
            x = [jnp.where(bits[3], x[i + 1], x[i]) for i in range(8)]
            terms = [a * b for a, b in zip(x, weights)]
            while len(terms) > 1:
                terms = [terms[i] + terms[i + 1] for i in range(0, len(terms), 2)]
            sums.append(terms[0].astype(F32))
        c, s = turn(square_ref[rows, :] * rate_ref[r])
        store(r, h, sums[0] * c - sums[1] * s, sums[0] * s + sums[1] * c)


SHIFT_LOW = 13


def focus_kernel(
    body_ref, head_ref, tail_ref, scale_ref, rate_ref, curve_ref, square_ref, taps_ref, table_ref,
    image_ref, padded_ref, wide_ref, re_ref, im_ref,
):
    for part in range(2):
        padded_ref[part, 0:HALO] = head_ref[part]
        padded_ref[part, HALO : HALO + OWN] = body_ref[part]
        padded_ref[part, HALO + OWN : 2 * HALO + OWN] = tail_ref[part]

    def store(r, h, re, im):
        rows = pl.ds(pl.multiple_of(r * LOW + 16 * h, 16), 16)
        wide_ref[0, rows, :] = re
        wide_ref[1, rows, :] = im

    def step(r, carry):
        migrate_rows(r, padded_ref, scale_ref, rate_ref, curve_ref, square_ref, taps_ref, store)
        return carry

    lax.fori_loop(0, OWN, step, 0)

    def back(k, carry):
        left = jnp.concatenate(
            [wide_ref[part, pl.ds(k, OWN, stride=LOW), :] for part in range(2)], axis=1
        ).astype(BF16)
        result = lax.dot_general(
            left, block_table(table_ref, k), (((1,), (1,)), ((), ())), preferred_element_type=F32
        )
        re_ref[k] = result[:, :EDGE]
        im_ref[k] = result[:, EDGE:]
        return carry

    lax.fori_loop(0, LOW, back, 0, unroll=4)
    low_transform(re_ref, im_ref, 1, low_store(re_ref, im_ref))

    def final(h, carry):
        columns = pl.ds(pl.multiple_of(h * EDGE, EDGE), EDGE)
        image_ref[0, :, columns] = re_ref[h].astype(BF16)
        image_ref[1, :, columns] = im_ref[h].astype(BF16)
        return carry

    lax.fori_loop(0, LOW, final, 0, unroll=4)


def focus(body, head, tail, scales, rates, curve, square, taps, table):
    vmem, smem = pl.BlockSpec(memory_space=pltpu.VMEM), pl.BlockSpec(memory_space=pltpu.SMEM)
    return pl.pallas_call(
        focus_kernel,
        out_shape=jax.ShapeDtypeStruct((2, OWN, PULSES), BF16),
        in_specs=[vmem, vmem, vmem, smem, smem, vmem, vmem, vmem, vmem],
        out_specs=vmem,
        scratch_shapes=[
            pltpu.VMEM((2, 2 * HALO + OWN + 8, LOW, EDGE), BF16),
            pltpu.VMEM((2, OWN * LOW, EDGE), F32),
            pltpu.VMEM((LOW, OWN, EDGE), F32),
            pltpu.VMEM((LOW, OWN, EDGE), F32),
        ],
        compiler_params=pltpu.CompilerParams(vmem_limit_bytes=48 << 20),
        name="focus",
    )(body, head, tail, scales, rates, curve, square, taps, table)


def shards(echoes, chirp_spectrum, fm_rate, range_scale, doppler_curve, kernels):
    me = lax.axis_index("wide") * lax.axis_size("narrow") + lax.axis_index("narrow")
    tables, twiddles = range_tables()
    azimuth = jnp.asarray(azimuth_tables())
    chirp = chirp_spectrum.reshape(2, EDGE, EDGE).transpose(0, 2, 1)
    got = compress(echoes, chirp, jnp.asarray(tables), jnp.asarray(twiddles))
    body = doppler_spectra(got, azimuth)
    head = lax.ppermute(body[:, OWN - HALO :], AXES, [(i, i + 1) for i in range(DEVICES - 1)])
    tail = lax.ppermute(body[:, :HALO], AXES, [(i + 1, i) for i in range(DEVICES - 1)])
    scales = lax.dynamic_slice_in_dim(range_scale, me * OWN, OWN)
    rates = lax.dynamic_slice_in_dim(fm_rate, me * OWN, OWN) * 0.5
    curve = doppler_curve.astype(F32).reshape(EDGE, LOW).T
    index = np.arange(PULSES)
    signed = (index + PULSES // 2) % PULSES - PULSES // 2
    square = jnp.asarray((signed * signed).astype(np.float32).reshape(EDGE, LOW).T)
    taps = jnp.broadcast_to(kernels.reshape(-1, 1, 1).astype(BF16), (PHASES * TAPS, 16, EDGE))
    return focus(body, head, tail, scales, rates, curve, square, taps, azimuth)


def solution(mesh):
    in_specs = (P(None, AXES, None), P(), P(), P(), P(), P())
    out_specs = P(None, AXES, None)
    return jax.shard_map(shards, mesh=mesh, in_specs=in_specs, out_specs=out_specs, check_vma=False)
```

```python
import functools
import math

import jax
import jax.numpy as jnp
import ml_dtypes
import numpy as np
from jax import lax
from jax.experimental import pallas as pl
from jax.experimental.pallas import tpu as pltpu
from jax.sharding import PartitionSpec as P

PULSES = 4096
BINS = 16384
EDGE = 128
LOW = 32
TAPS = 8
PHASES = 8
HALO = 16
DEVICES = 256
OWN = BINS // DEVICES
ROWS = PULSES // DEVICES
AXES = ("wide", "narrow")
F32 = jnp.float32
BF16 = jnp.bfloat16


def roots(product, total):
    angles = 2.0 * np.pi / total * (product % total)
    return np.cos(angles), np.sin(angles)


def range_tables():
    count = np.arange(EDGE)
    c, s = roots(np.outer(count, count), EDGE)
    c, s = c / math.sqrt(EDGE), s / math.sqrt(EDGE)
    fwd_left = np.block([[c, s], [-s, c]])
    inv_left = np.block([[c, -s], [s, c]])
    tables = np.stack([fwd_left, fwd_left.T, inv_left.T, inv_left])
    tc, ts = roots(np.outer(count, count), BINS)
    return tables.astype(ml_dtypes.bfloat16), np.stack([tc, ts]).astype(np.float32)


def azimuth_tables():
    low = np.arange(LOW)[:, None, None]
    n = np.arange(EDGE)[None, :, None]
    j = np.arange(EDGE)[None, None, :]
    c, s = roots(n * (low + LOW * j), PULSES)
    return (np.stack([c, s], axis=1) / math.sqrt(PULSES)).astype(ml_dtypes.bfloat16)


def fft(values, sign):
    count = len(values)
    if count == 1:
        return values
    even, odd = fft(values[0::2], sign), fft(values[1::2], sign)
    half = count // 2
    out = [None] * count
    for k in range(half):
        (ar, ai), (br, bi) = even[k], odd[k]
        if k == 0:
            tr, ti = br, bi
        elif 4 * k == count:
            tr, ti = (-bi, br) if sign > 0 else (bi, -br)
        else:
            angle = 2.0 * math.pi * k / count
            c, s = math.cos(angle), sign * math.sin(angle)
            if 8 * k == count:
                tr, ti = (br - bi * (1 if sign > 0 else -1)) * c, (bi + br * (1 if sign > 0 else -1)) * c
            else:
                tr, ti = br * c - bi * s, br * s + bi * c
        out[k] = (ar + tr, ai + ti)
        out[k + half] = (ar - tr, ai - ti)
    return out


def dot(a, b):
    return jnp.dot(a, b, preferred_element_type=F32)


MESH_IDS = pl.DeviceIdType.MESH


def place():
    wide, narrow = lax.axis_index("wide"), lax.axis_index("narrow")
    return wide % 4, (narrow // 2) * 2 + wide // 32, (wide // 4) % 8, narrow % 2


def device_at(x, y, z, core):
    return ((y % 2) * 8 + z) * 4 + x, (y // 2) * 2 + core


def signal(semaphore, x, y, z, core):
    wide, narrow = device_at(x, y, z, core)
    pl.semaphore_signal(
        semaphore, inc=1, device_id={"wide": wide, "narrow": narrow}, device_id_type=MESH_IDS
    )


def split_pairs(got_ref, re_ref, im_ref):
    half = EDGE // 2
    low_half = lax.broadcasted_iota(jnp.int32, (ROWS, EDGE), 1) < half

    def step(m, carry):
        for g in range(half // ROWS):
            near = got_ref[m * 8 + g].astype(F32)
            far = got_ref[m * 8 + 4 + g].astype(F32)
            rows = pl.ds(g * ROWS, ROWS)
            re_ref[m, rows, :] = jnp.where(low_half, near, pltpu.roll(far, half, 1))
            im_ref[m, rows, :] = jnp.where(low_half, pltpu.roll(near, half, 1), far)
        return carry

    lax.fori_loop(0, LOW, step, 0, unroll=2)


def low_transform(re_ref, im_ref, sign, block, store):
    def step(g, carry):
        rows = pl.ds(pl.multiple_of(g * block, block), block)
        values = fft([(re_ref[m, rows, :], im_ref[m, rows, :]) for m in range(LOW)], sign)
        for k, (re, im) in enumerate(values):
            store(k, rows, re, im)
        return carry

    lax.fori_loop(0, EDGE // 2 // block, step, 0)


def low_store(re_ref, im_ref):
    def store(k, rows, re, im):
        re_ref[k, rows, :] = re
        im_ref[k, rows, :] = im

    return store


def block_table(table_ref, k):
    c, s = table_ref[k, 0], table_ref[k, 1]
    return jnp.concatenate(
        [jnp.concatenate([c, -s], axis=1), jnp.concatenate([s, c], axis=1)], axis=0
    )


def turn(turns):
    x = turns - jnp.round(turns)
    y = x * x
    c = jnp.full_like(x, COS_TERMS[-1])
    for term in COS_TERMS[-2::-1]:
        c = c * y + term
    s = jnp.full_like(x, SIN_TERMS[-1])
    for term in SIN_TERMS[-2::-1]:
        s = s * y + term
    return c, s * x


def fitted_terms():
    x = np.cos(np.pi * (np.arange(400) + 0.5) / 800) * 0.5
    y = x * x
    powers = np.stack([y**i for i in range(6)], axis=1)
    c = np.linalg.lstsq(powers, np.cos(2 * np.pi * x), rcond=None)[0]
    s = np.linalg.lstsq(powers * x[:, None], np.sin(2 * np.pi * x), rcond=None)[0]
    return [float(v) for v in c], [float(v) for v in s]


COS_TERMS, SIN_TERMS = fitted_terms()


def order_curve(angle_ref, curve_ref):
    values = angle_ref[...].astype(F32)
    upper = jnp.floor(values * (1.0 / 64.0))
    lower = values - 64.0 * upper
    row = lax.broadcasted_iota(jnp.int32, (LOW, EDGE), 0)
    lane = lax.broadcasted_iota(jnp.int32, (LOW, EDGE), 1)
    total = jnp.zeros((LOW, EDGE), F32)
    for digit, size in ((upper, 64.0), (lower, 1.0)):
        digit = digit.astype(BF16)
        for i in range(EDGE // LOW):
            pick = jnp.where(lane == LOW * i + row, 1.0, 0.0).astype(BF16)
            part = lax.dot_general(pick, digit, (((1,), (1,)), ((), ())), preferred_element_type=F32)
            place_at = jnp.where(lane == 4 * row + i, 1.0, 0.0).astype(BF16)
            total = total + size * dot(part.astype(BF16), place_at)
    curve_ref[...] = total


def prepare_rows(r, scale, rate, curve_ref, square_ref, taps_ref, bit_ref, weight_ref, phase_ref):
    offset = jnp.where(scale < 0, 8.0 * SHIFT_LOW, 0.0).astype(F32)
    scale = scale.astype(F32) * (1.0 / 4096.0)
    for h in range(2):
        rows = pl.ds(16 * h, 16)
        level = (jnp.floor(curve_ref[rows, :] * scale) + offset).astype(BF16)
        bits = []
        for i, weight in enumerate((64, 32, 16, 8, 4, 2, 1)):
            bit = level >= jnp.asarray(weight, BF16)
            bits.append(bit)
            if i < 4:
                bit_ref[r, i, rows, :] = jnp.where(bit, jnp.asarray(1, BF16), jnp.asarray(0, BF16))
            if weight > 1:
                level = jnp.where(bit, level - jnp.asarray(weight, BF16), level)
        for t in range(TAPS):
            level4 = [jnp.where(bits[6], taps_ref[(2 * i + 1) * TAPS + t], taps_ref[2 * i * TAPS + t]) for i in range(4)]
            level2 = [jnp.where(bits[5], level4[2 * i + 1], level4[2 * i]) for i in range(2)]
            weight_ref[r, t, rows, :] = jnp.where(bits[4], level2[1], level2[0])
        c, s = turn(square_ref[rows, :] * rate)
        phase_ref[0, r, rows, :] = c
        phase_ref[1, r, rows, :] = s


def migrate_rows(r, scale, padded_ref, bit_ref, weight_ref, phase_ref, store):
    first = r + HALO - 3 - jnp.where(scale < 0, SHIFT_LOW, 0)
    for h in range(2):
        rows = pl.ds(16 * h, 16)
        bits = [bit_ref[r, i, rows, :] > jnp.asarray(0, BF16) for i in range(4)]
        sums = []
        for part in range(2):
            x = [padded_ref[part, first + i, rows, :] for i in range(21)]
            x = [jnp.where(bits[0], x[i + 8], x[i]) if i < 13 else x[i] for i in range(15)]
            x = [jnp.where(bits[1], x[i + 4], x[i]) for i in range(11)]
            x = [jnp.where(bits[2], x[i + 2], x[i]) for i in range(9)]
            x = [jnp.where(bits[3], x[i + 1], x[i]) for i in range(8)]
            terms = [x[t] * weight_ref[r, t, rows, :] for t in range(TAPS)]
            while len(terms) > 1:
                terms = [terms[i] + terms[i + 1] for i in range(0, len(terms), 2)]
            sums.append(terms[0].astype(F32))
        c, s = phase_ref[0, r, rows, :], phase_ref[1, r, rows, :]
        store(r, h, sums[0] * c - sums[1] * s, sums[0] * s + sums[1] * c)


SHIFT_LOW = 13


def main_kernel(
    echo_hbm, chirp_hbm, table_hbm, twiddle_hbm, azimuth_hbm, scale_hbm, rate_hbm, angle_hbm, square_hbm, kernel_hbm,
    image_ref,
    echo_ref, line_ref, table_ref, twiddle_ref, azimuth_ref, scale_ref, rate_ref, angle_ref, square_ref, kernel_ref,
    chirp_ref, curve_ref, taps_ref, bit_ref, weight_ref, phase_ref,
    send_ref, got_ref, wide_ref, turned_ref, re_ref, im_ref, padded_ref, head_ref, tail_ref,
    load_sems, y_sem, z_sem, send_sem, recv_sem, own_sem, halo_send, halo_recv,
):
    x, y, z, core = place()
    wide, narrow = device_at(x, y, z, core)
    me = wide * 4 + narrow

    pieces = 4
    echo_loads = []
    for i in range(pieces):
        columns = pl.ds(i * (BINS // pieces), BINS // pieces)
        load = pltpu.make_async_copy(
            echo_hbm.at[:, :, columns], echo_ref.at[:, :, columns], load_sems.at[i]
        )
        load.start()
        echo_loads.append(load)
    own_rows = pl.ds(pl.multiple_of(me // 16 * 8, 8), 8)
    loads = []
    for i, (source, target) in enumerate(
        (
            (chirp_hbm, line_ref), (table_hbm, table_ref), (twiddle_hbm, twiddle_ref),
            (azimuth_hbm, azimuth_ref), (angle_hbm, angle_ref), (square_hbm, square_ref), (kernel_hbm, kernel_ref),
            (scale_hbm.at[own_rows], scale_ref), (rate_hbm.at[own_rows], rate_ref),
        )
    ):
        load = pltpu.make_async_copy(source, target, load_sems.at[pieces + i])
        load.start()
        loads.append(load)

    barrier = pltpu.get_barrier_semaphore()
    for i in range(1, 8):
        signal(barrier, (x + i // 2) % 4, y, z, (core + i) % 2)
    for i in range(1, 4):
        signal(barrier, x, (y + i) % 4, z, core)
    for i in range(1, 8):
        signal(barrier, x, y, (z + i) % 8, core)

    def spread(m, carry):
        columns = pl.ds(pl.multiple_of(m * EDGE, EDGE), EDGE)
        for part in range(2):
            block = echo_ref[part, :, columns].astype(F32)
            wide_ref[part, pl.ds(pl.multiple_of(m * ROWS, ROWS), ROWS), :] = block
        return carry

    for i in range(pieces):
        echo_loads[i].wait()
        lax.fori_loop(i * (EDGE // pieces), (i + 1) * (EDGE // pieces), spread, 0, unroll=8)
    for load in loads[:3]:
        load.wait()

    def lay(j, carry):
        for part in range(2):
            chirp_ref[part, pl.ds(j, 1), :] = line_ref[part : part + 1, pl.ds(pl.multiple_of(j * EDGE, EDGE), EDGE)]
        return carry

    lax.fori_loop(0, EDGE, lay, 0, unroll=8)
    for part in range(2):
        chirp_ref[part] = chirp_ref[part].T

    pl.semaphore_wait(barrier, 17)
    for i in range(1, 4):
        signal(y_sem, x, (y + i) % 4, z, core)
    tc, ts = twiddle_ref[0], twiddle_ref[1]

    def pair(i, carry):
        b = 2 * i
        signals = jnp.concatenate(
            [
                jnp.concatenate(
                    [wide_ref[part, pl.ds(b + h, EDGE, stride=ROWS), :] for h in range(2)], axis=1
                )
                for part in range(2)
            ],
            axis=0,
        ).astype(BF16)
        first = dot(table_ref[0], signals)
        rows = []
        for h in range(2):
            re, im = first[:EDGE, h * EDGE : (h + 1) * EDGE], first[EDGE:, h * EDGE : (h + 1) * EDGE]
            rows.append(jnp.concatenate([re * tc + im * ts, im * tc - re * ts], axis=1))
        spectrum = dot(jnp.concatenate(rows, axis=0).astype(BF16), table_ref[1])
        rows = []
        for h in range(2):
            re, im = spectrum[h * EDGE : (h + 1) * EDGE, :EDGE], spectrum[h * EDGE : (h + 1) * EDGE, EDGE:]
            rows.append(
                jnp.concatenate(
                    [re * chirp_ref[0] - im * chirp_ref[1], re * chirp_ref[1] + im * chirp_ref[0]], axis=1
                )
            )
        back = dot(jnp.concatenate(rows, axis=0).astype(BF16), table_ref[2])
        columns = []
        for h in range(2):
            re, im = back[h * EDGE : (h + 1) * EDGE, :EDGE], back[h * EDGE : (h + 1) * EDGE, EDGE:]
            columns.append(jnp.concatenate([re * tc - im * ts, im * tc + re * ts], axis=0))
        result = dot(table_ref[3], jnp.concatenate(columns, axis=1).astype(BF16))
        for h in range(2):
            for part in range(2):
                turned_ref[part, pl.ds(b + h, EDGE, stride=ROWS), :] = result[
                    part * EDGE : (part + 1) * EDGE, h * EDGE : (h + 1) * EDGE
                ]
        return carry

    lax.fori_loop(0, ROWS // 4, pair, 0, unroll=UNROLL)
    pl.semaphore_wait(y_sem, 3)
    for i in range(1, 8):
        signal(z_sem, x, y, (z + i) % 8, core)
    lax.fori_loop(ROWS // 4, ROWS // 2, pair, 0, unroll=UNROLL)
    low_half = lax.broadcasted_iota(jnp.int32, (ROWS, EDGE), 1) < EDGE // 2

    def pack(u, carry):
        rows = pl.ds(pl.multiple_of(u * ROWS, ROWS), ROWS)
        re, im = turned_ref[0, rows, :], turned_ref[1, rows, :]
        send_ref[2 * u] = jnp.where(low_half, re, pltpu.roll(im, EDGE // 2, 1)).astype(BF16)
        send_ref[2 * u + 1] = jnp.where(low_half, pltpu.roll(re, EDGE // 2, 1), im).astype(BF16)
        return carry

    lax.fori_loop(0, EDGE, pack, 0, unroll=8)
    pl.semaphore_wait(z_sem, 7)

    def start(to_wide, to_narrow, to):
        pltpu.make_async_remote_copy(
            send_ref.at[to], got_ref.at[me], send_sem, recv_sem,
            device_id={"wide": to_wide, "narrow": to_narrow}, device_id_type=MESH_IDS,
        ).start()

    def spread_out(t, carry):
        z_step = jnp.where(core == 0, t % 8, (8 - t % 8) % 8)
        x_step = (t // 8 + z_step) % 4
        y_step = (t // 32 + z_step // 2) % 4
        to_wide, to_narrow = device_at((x + x_step) % 4, (y + y_step) % 4, (z + z_step) % 8, 0)
        to = to_wide * 4 + to_narrow
        start(to_wide, to_narrow, to)
        start(to_wide, to_narrow + 1, to + 1)
        return carry

    start(wide, narrow + 1 - 2 * core, me + 1 - 2 * core)
    lax.fori_loop(1, EDGE, spread_out, 0)
    own = pltpu.make_async_copy(send_ref.at[me], got_ref.at[me], own_sem)
    own.start()
    own.wait()

    for load in loads[3:]:
        load.wait()
    order_curve(angle_ref, curve_ref)
    for i in range(PHASES * TAPS):
        tap = kernel_ref[i // TAPS : i // TAPS + 1, i % TAPS : i % TAPS + 1]
        taps_ref[i] = jnp.broadcast_to(tap, (16, EDGE)).astype(BF16)
    scale_row, scale_column = me // 2 % 8, me % 2 * OWN

    def prepare(r, carry):
        prepare_rows(
            r, scale_ref[scale_row, scale_column + r], rate_ref[scale_row, scale_column + r] * 0.5,
            curve_ref, square_ref, taps_ref, bit_ref, weight_ref, phase_ref,
        )
        return carry

    lax.fori_loop(0, OWN, prepare, 0)
    others = pltpu.make_async_remote_copy(
        send_ref.at[pl.ds(0, DEVICES - 1)], got_ref.at[pl.ds(0, DEVICES - 1)], send_sem, recv_sem,
        device_id={"wide": wide, "narrow": (narrow + 1) % 4}, device_id_type=MESH_IDS,
    )
    others.wait_send()
    others.wait_recv()


    half = EDGE // 2
    split_pairs(got_ref, re_ref, im_ref)
    low_transform(re_ref, im_ref, -1, 8, low_store(re_ref, im_ref))

    def high(k, carry):
        re, im = re_ref[k], im_ref[k]
        left = jnp.concatenate(
            [re, pltpu.roll(re, half, 1), im, pltpu.roll(im, half, 1)], axis=0
        ).astype(BF16)
        result = lax.dot_general(
            left, block_table(azimuth_ref, k), (((0,), (0,)), ((), ())), preferred_element_type=F32
        )
        for part in range(2):
            wide_ref[part, pl.ds(k, OWN, stride=LOW), :] = result[:OWN, part * EDGE : (part + 1) * EDGE]
        return carry

    halos = []
    for h in range(2):
        lax.fori_loop(16 * h, 16 * h + 16, high, 0, unroll=4)

        def narrowed(r, carry, h=h):
            rows = pl.ds(pl.multiple_of(r * LOW + 16 * h, 16), 16)
            for part in range(2):
                padded_ref[part, HALO + r, 16 * h : 16 * h + 16, :] = wide_ref[part, rows, :].astype(BF16)
            return carry

        lax.fori_loop(0, OWN, narrowed, 0, unroll=8)
        k_rows = pl.ds(16 * h, 16)
        for side in range(2):
            other = (me + 1 - 2 * side + DEVICES) % DEVICES
            first = OWN if side == 0 else HALO
            target = head_ref if side == 0 else tail_ref
            halo = pltpu.make_async_remote_copy(
                padded_ref.at[:, pl.ds(first, HALO), k_rows, :], target.at[:, :, k_rows, :],
                halo_send.at[2 * h + side], halo_recv.at[2 * h + side],
                device_id={"wide": other // 4, "narrow": other % 4}, device_id_type=MESH_IDS,
            )
            halo.start()
            halos.append(halo)

    def store(r, h, re, im):
        rows = pl.ds(pl.multiple_of(r * LOW + 16 * h, 16), 16)
        turned_ref[0, rows, :] = re
        turned_ref[1, rows, :] = im

    def migrate(r):
        migrate_rows(
            r, scale_ref[scale_row, scale_column + r], padded_ref, bit_ref, weight_ref, phase_ref, store
        )

    def inner(r, carry):
        migrate(r)
        return carry

    lax.fori_loop(HALO, OWN - HALO, inner, 0)
    for halo in halos:
        halo.wait()

    def edge(r, carry):
        for part in range(2):
            padded_ref[part, r] = jnp.where(me == 0, jnp.zeros((LOW, EDGE), BF16), head_ref[part, r])
            padded_ref[part, HALO + OWN + r] = jnp.where(
                me == DEVICES - 1, jnp.zeros((LOW, EDGE), BF16), tail_ref[part, r]
            )
        return carry

    lax.fori_loop(0, HALO, edge, 0)

    def outer(i, carry):
        migrate(jnp.where(i < HALO, i, i + OWN - 2 * HALO))
        return carry

    lax.fori_loop(0, 2 * HALO, outer, 0)

    def back(k, carry):
        left = jnp.concatenate(
            [turned_ref[part, pl.ds(k, OWN, stride=LOW), :] for part in range(2)], axis=1
        ).astype(BF16)
        result = lax.dot_general(
            left, block_table(azimuth_ref, k), (((1,), (1,)), ((), ())), preferred_element_type=F32
        )
        re_ref[k] = result[:, :EDGE]
        im_ref[k] = result[:, EDGE:]
        return carry

    lax.fori_loop(0, LOW, back, 0, unroll=4)

    def finish(h, rows, re, im):
        image_ref[0, rows, h * EDGE : (h + 1) * EDGE] = re.astype(BF16)
        image_ref[1, rows, h * EDGE : (h + 1) * EDGE] = im.astype(BF16)

    low_transform(re_ref, im_ref, 1, 16, finish)


UNROLL = 2
VMEM_BYTES = 63 << 20


def focused_image(*operands):
    big = pltpu.VMEM((2, EDGE * ROWS, EDGE), F32)
    scratch = [pltpu.VMEM(operand.shape, operand.dtype) for operand in operands[:5]]
    scratch += [pltpu.SMEM((8, EDGE), jnp.int32), pltpu.SMEM((8, EDGE), F32)]
    scratch += [pltpu.VMEM(operand.shape, operand.dtype) for operand in operands[7:]]
    scratch += [
        pltpu.VMEM((2, EDGE, EDGE), F32),
        pltpu.VMEM((LOW, EDGE), F32),
        pltpu.VMEM((PHASES * TAPS, 16, EDGE), BF16),
        pltpu.VMEM((OWN, 4, LOW, EDGE), BF16),
        pltpu.VMEM((OWN, TAPS, LOW, EDGE), BF16),
        pltpu.VMEM((2, OWN, LOW, EDGE), F32),
        pltpu.VMEM((DEVICES, ROWS, EDGE), BF16),
        pltpu.VMEM((DEVICES, ROWS, EDGE), BF16),
        big,
        big,
        pltpu.VMEM((LOW, EDGE // 2, EDGE), F32),
        pltpu.VMEM((LOW, EDGE // 2, EDGE), F32),
        pltpu.VMEM((2, 2 * HALO + OWN + 8, LOW, EDGE), BF16),
        pltpu.VMEM((2, HALO, LOW, EDGE), BF16),
        pltpu.VMEM((2, HALO, LOW, EDGE), BF16),
        pltpu.SemaphoreType.DMA((13,)),
        pltpu.SemaphoreType.REGULAR,
        pltpu.SemaphoreType.REGULAR,
        pltpu.SemaphoreType.DMA,
        pltpu.SemaphoreType.DMA,
        pltpu.SemaphoreType.DMA,
        pltpu.SemaphoreType.DMA((4,)),
        pltpu.SemaphoreType.DMA((4,)),
    ]
    return pl.pallas_call(
        main_kernel,
        out_shape=jax.ShapeDtypeStruct((2, OWN, PULSES), BF16),
        in_specs=[pl.BlockSpec(memory_space=pl.ANY)] * 10,
        out_specs=pl.BlockSpec(memory_space=pltpu.VMEM),
        scratch_shapes=scratch,
        compiler_params=pltpu.CompilerParams(
            collective_id=0, has_side_effects=True, vmem_limit_bytes=VMEM_BYTES
        ),
        name="focused_image",
    )(*operands)


def shards(echoes, chirp_spectrum, fm_rate, range_scale, doppler_curve, kernels):
    tables, twiddles = range_tables()
    index = np.arange(PULSES)
    signed = (index + PULSES // 2) % PULSES - PULSES // 2
    square = np.ascontiguousarray((signed * signed).astype(np.float32).reshape(EDGE, LOW).T)
    return focused_image(
        echoes, chirp_spectrum, jnp.asarray(tables), jnp.asarray(twiddles), jnp.asarray(azimuth_tables()),
        range_scale.reshape(EDGE, EDGE), fm_rate.reshape(EDGE, EDGE),
        doppler_curve.reshape(LOW, EDGE), jnp.asarray(square), kernels,
    )


def solution(mesh):
    in_specs = (P(None, AXES, None), P(), P(), P(), P(), P())
    out_specs = P(None, AXES, None)
    return jax.shard_map(shards, mesh=mesh, in_specs=in_specs, out_specs=out_specs, check_vma=False)
```

```python
import functools
import math

import jax
import jax.numpy as jnp
import ml_dtypes
import numpy as np
from jax import lax
from jax.experimental import pallas as pl
from jax.experimental.pallas import tpu as pltpu
from jax.sharding import PartitionSpec as P

PULSES = 4096
BINS = 16384
EDGE = 128
LOW = 32
TAPS = 8
PHASES = 8
HALO = 16
DEVICES = 256
OWN = BINS // DEVICES
ROWS = PULSES // DEVICES
AXES = ("wide", "narrow")
F32 = jnp.float32
BF16 = jnp.bfloat16


def roots(product, total):
    angles = 2.0 * np.pi / total * (product % total)
    return np.cos(angles), np.sin(angles)


def range_tables():
    count = np.arange(EDGE)
    c, s = roots(np.outer(count, count), EDGE)
    c, s = c / math.sqrt(EDGE), s / math.sqrt(EDGE)
    fwd_left = np.block([[c, s], [-s, c]])
    inv_left = np.block([[c, -s], [s, c]])
    tables = np.stack([fwd_left, fwd_left.T, inv_left.T, inv_left])
    tc, ts = roots(np.outer(count, count), BINS)
    return tables.astype(ml_dtypes.bfloat16), np.stack([tc, ts]).astype(np.float32)


def azimuth_tables():
    low = np.arange(LOW)[:, None, None]
    n = np.arange(EDGE)[None, :, None]
    j = np.arange(EDGE)[None, None, :]
    c, s = roots(n * (low + LOW * j), PULSES)
    forward = np.concatenate(
        [np.concatenate([c, -s], axis=2), np.concatenate([s, c], axis=2)], axis=1
    ) / math.sqrt(PULSES)
    inverse = np.ascontiguousarray(forward.transpose(0, 2, 1))
    return forward.astype(ml_dtypes.bfloat16), inverse.astype(ml_dtypes.bfloat16)


def fft(values, sign):
    count = len(values)
    if count == 1:
        return values
    even, odd = fft(values[0::2], sign), fft(values[1::2], sign)
    half = count // 2
    out = [None] * count
    for k in range(half):
        (ar, ai), (br, bi) = even[k], odd[k]
        if k == 0:
            tr, ti = br, bi
        elif 4 * k == count:
            tr, ti = (-bi, br) if sign > 0 else (bi, -br)
        else:
            angle = 2.0 * math.pi * k / count
            c, s = math.cos(angle), sign * math.sin(angle)
            if 8 * k == count:
                tr, ti = (br - bi * (1 if sign > 0 else -1)) * c, (bi + br * (1 if sign > 0 else -1)) * c
            else:
                tr, ti = br * c - bi * s, br * s + bi * c
        out[k] = (ar + tr, ai + ti)
        out[k + half] = (ar - tr, ai - ti)
    return out


def dot(a, b):
    return jnp.dot(a, b, preferred_element_type=F32)


MESH_IDS = pl.DeviceIdType.MESH


def place():
    wide, narrow = lax.axis_index("wide"), lax.axis_index("narrow")
    return wide % 4, (narrow // 2) * 2 + wide // 32, (wide // 4) % 8, narrow % 2


def device_at(x, y, z, core):
    return ((y % 2) * 8 + z) * 4 + x, (y // 2) * 2 + core


def signal(semaphore, x, y, z, core):
    wide, narrow = device_at(x, y, z, core)
    pl.semaphore_signal(
        semaphore, inc=1, device_id={"wide": wide, "narrow": narrow}, device_id_type=MESH_IDS
    )


def split_pairs(got_ref, re_ref, im_ref):
    half = EDGE // 2
    low_half = lax.broadcasted_iota(jnp.int32, (ROWS, EDGE), 1) < half

    def step(m, carry):
        for g in range(half // ROWS):
            near = got_ref[m * 8 + g].astype(F32)
            far = got_ref[m * 8 + 4 + g].astype(F32)
            rows = pl.ds(g * ROWS, ROWS)
            re_ref[m, rows, :] = jnp.where(low_half, near, pltpu.roll(far, half, 1))
            im_ref[m, rows, :] = jnp.where(low_half, pltpu.roll(near, half, 1), far)
        return carry

    lax.fori_loop(0, LOW, step, 0, unroll=2)


def low_transform(re_ref, im_ref, sign, block, store, first=0, count=8, stride=8):
    def step(g, carry):
        rows = pl.ds(pl.multiple_of(first + g * stride, block), block)
        values = fft([(re_ref[m, rows, :], im_ref[m, rows, :]) for m in range(LOW)], sign)
        for k, (re, im) in enumerate(values):
            store(k, rows, re, im)
        return carry

    lax.fori_loop(0, count, step, 0)


def low_store(re_ref, im_ref):
    def store(k, rows, re, im):
        re_ref[k, rows, :] = re
        im_ref[k, rows, :] = im

    return store


def turn(turns):
    x = turns - jnp.round(turns)
    y = x * x
    c = jnp.full_like(x, COS_TERMS[-1])
    for term in COS_TERMS[-2::-1]:
        c = c * y + term
    s = jnp.full_like(x, SIN_TERMS[-1])
    for term in SIN_TERMS[-2::-1]:
        s = s * y + term
    return c, s * x


def fitted_terms():
    x = np.cos(np.pi * (np.arange(400) + 0.5) / 800) * 0.5
    y = x * x
    powers = np.stack([y**i for i in range(6)], axis=1)
    c = np.linalg.lstsq(powers, np.cos(2 * np.pi * x), rcond=None)[0]
    s = np.linalg.lstsq(powers * x[:, None], np.sin(2 * np.pi * x), rcond=None)[0]
    return [float(v) for v in c], [float(v) for v in s]


COS_TERMS, SIN_TERMS = fitted_terms()


def order_curve(angle_ref, curve_ref):
    values = angle_ref[...].astype(F32)
    upper = jnp.floor(values * (1.0 / 64.0))
    lower = values - 64.0 * upper
    row = lax.broadcasted_iota(jnp.int32, (LOW, EDGE), 0)
    lane = lax.broadcasted_iota(jnp.int32, (LOW, EDGE), 1)
    total = jnp.zeros((LOW, EDGE), F32)
    for digit, size in ((upper, 64.0), (lower, 1.0)):
        digit = digit.astype(BF16)
        for i in range(EDGE // LOW):
            pick = jnp.where(lane == LOW * i + row, 1.0, 0.0).astype(BF16)
            part = lax.dot_general(pick, digit, (((1,), (1,)), ((), ())), preferred_element_type=F32)
            place_at = jnp.where(lane == 4 * row + i, 1.0, 0.0).astype(BF16)
            total = total + size * dot(part.astype(BF16), place_at)
    curve_ref[...] = total


def prepare_rows(r, scale, rate, curve_ref, square_ref, taps_ref, bit_ref, weight_ref, phase_ref):
    offset = jnp.where(scale < 0, 8.0 * SHIFT_LOW, 0.0).astype(F32)
    scale = scale.astype(F32) * (1.0 / 4096.0)
    for h in range(2):
        rows = pl.ds(16 * h, 16)
        level = (jnp.floor(curve_ref[rows, :] * scale) + offset).astype(BF16)
        bits = []
        for i, weight in enumerate((64, 32, 16, 8, 4, 2, 1)):
            bit = level >= jnp.asarray(weight, BF16)
            bits.append(bit)
            if i < 4:
                bit_ref[r, i, rows, :] = jnp.where(bit, jnp.asarray(1, BF16), jnp.asarray(0, BF16))
            if weight > 1:
                level = jnp.where(bit, level - jnp.asarray(weight, BF16), level)
        for t in range(TAPS):
            level4 = [jnp.where(bits[6], taps_ref[(2 * i + 1) * TAPS + t], taps_ref[2 * i * TAPS + t]) for i in range(4)]
            level2 = [jnp.where(bits[5], level4[2 * i + 1], level4[2 * i]) for i in range(2)]
            weight_ref[r, t, rows, :] = jnp.where(bits[4], level2[1], level2[0])
        c, s = turn(square_ref[rows, :] * rate)
        phase_ref[0, r, rows, :] = c
        phase_ref[1, r, rows, :] = s


def migrate_rows(r, scale, halves, padded_ref, bit_ref, weight_ref, phase_ref, store):
    first = r + HALO - 3 - jnp.where(scale < 0, SHIFT_LOW, 0)
    for h in halves:
        rows = pl.ds(16 * h, 16)
        bits = [bit_ref[r, i, rows, :] > jnp.asarray(0, BF16) for i in range(4)]
        sums = []
        for part in range(2):
            x = [padded_ref[part, first + i, rows, :] for i in range(21)]
            x = [jnp.where(bits[0], x[i + 8], x[i]) if i < 13 else x[i] for i in range(15)]
            x = [jnp.where(bits[1], x[i + 4], x[i]) for i in range(11)]
            x = [jnp.where(bits[2], x[i + 2], x[i]) for i in range(9)]
            x = [jnp.where(bits[3], x[i + 1], x[i]) for i in range(8)]
            terms = [x[t] * weight_ref[r, t, rows, :] for t in range(TAPS)]
            while len(terms) > 1:
                terms = [terms[i] + terms[i + 1] for i in range(0, len(terms), 2)]
            sums.append(terms[0].astype(F32))
        c, s = phase_ref[0, r, rows, :], phase_ref[1, r, rows, :]
        store(r, h, sums[0] * c - sums[1] * s, sums[0] * s + sums[1] * c)


SHIFT_LOW = 13


def main_kernel(
    echo_hbm, chirp_hbm, table_hbm, twiddle_hbm, azimuth_hbm, scale_hbm, rate_hbm, angle_hbm, square_hbm, kernel_hbm, inverse_hbm,
    image_hbm,
    echo_ref, line_ref, table_ref, twiddle_ref, azimuth_ref, scale_ref, rate_ref, angle_ref, square_ref, kernel_ref, inverse_ref,
    image_ref,
    chirp_ref, curve_ref, taps_ref, bit_ref, weight_ref, phase_ref,
    send_ref, got_ref, wide_ref, turned_ref, re_ref, im_ref, padded_ref, head_ref, tail_ref,
    load_sems, y_sem, z_sem, send_sem, recv_sem, own_sem, halo_send, halo_recv, image_sems,
):
    x, y, z, core = place()
    wide, narrow = device_at(x, y, z, core)
    me = wide * 4 + narrow

    pieces = 4
    echo_loads = []
    for i in range(pieces):
        columns = pl.ds(i * (BINS // pieces), BINS // pieces)
        load = pltpu.make_async_copy(
            echo_hbm.at[:, :, columns], echo_ref.at[:, :, columns], load_sems.at[i]
        )
        load.start()
        echo_loads.append(load)
    own_rows = pl.ds(pl.multiple_of(me // 16 * 8, 8), 8)
    loads = []
    for i, (source, target) in enumerate(
        (
            (chirp_hbm, line_ref), (table_hbm, table_ref), (twiddle_hbm, twiddle_ref),
            (angle_hbm, angle_ref), (square_hbm, square_ref), (kernel_hbm, kernel_ref),
            (scale_hbm.at[own_rows], scale_ref), (rate_hbm.at[own_rows], rate_ref),
            (azimuth_hbm, azimuth_ref), (inverse_hbm, inverse_ref),
        )
    ):
        load = pltpu.make_async_copy(source, target, load_sems.at[pieces + i])
        if i < 8:
            load.start()
        loads.append(load)

    barrier = pltpu.get_barrier_semaphore()
    for i in range(1, 8):
        signal(barrier, (x + i // 2) % 4, y, z, (core + i) % 2)
    for i in range(1, 4):
        signal(barrier, x, (y + i) % 4, z, core)
    for i in range(1, 8):
        signal(barrier, x, y, (z + i) % 8, core)

    def spread(m, carry):
        columns = pl.ds(pl.multiple_of(m * EDGE, EDGE), EDGE)
        for part in range(2):
            block = echo_ref[part, :, columns].astype(F32)
            wide_ref[part, pl.ds(pl.multiple_of(m * ROWS, ROWS), ROWS), :] = block
        return carry

    for i in range(pieces):
        echo_loads[i].wait()
        lax.fori_loop(i * (EDGE // pieces), (i + 1) * (EDGE // pieces), spread, 0, unroll=8)
    for load in loads[:3]:
        load.wait()
    for load in loads[8:]:
        load.start()

    def lay(j, carry):
        for part in range(2):
            chirp_ref[part, pl.ds(j, 1), :] = line_ref[part : part + 1, pl.ds(pl.multiple_of(j * EDGE, EDGE), EDGE)]
        return carry

    lax.fori_loop(0, EDGE, lay, 0, unroll=8)
    for part in range(2):
        chirp_ref[part] = chirp_ref[part].T

    pl.semaphore_wait(barrier, 17)
    for i in range(1, 4):
        signal(y_sem, x, (y + i) % 4, z, core)
    tc, ts = twiddle_ref[0], twiddle_ref[1]

    def pair(i, carry):
        b = 2 * i
        signals = jnp.concatenate(
            [
                jnp.concatenate(
                    [wide_ref[part, pl.ds(b + h, EDGE, stride=ROWS), :] for h in range(2)], axis=1
                )
                for part in range(2)
            ],
            axis=0,
        ).astype(BF16)
        first = dot(table_ref[0], signals)
        rows = []
        for h in range(2):
            re, im = first[:EDGE, h * EDGE : (h + 1) * EDGE], first[EDGE:, h * EDGE : (h + 1) * EDGE]
            rows.append(jnp.concatenate([re * tc + im * ts, im * tc - re * ts], axis=1))
        spectrum = dot(jnp.concatenate(rows, axis=0).astype(BF16), table_ref[1])
        rows = []
        for h in range(2):
            re, im = spectrum[h * EDGE : (h + 1) * EDGE, :EDGE], spectrum[h * EDGE : (h + 1) * EDGE, EDGE:]
            rows.append(
                jnp.concatenate(
                    [re * chirp_ref[0] - im * chirp_ref[1], re * chirp_ref[1] + im * chirp_ref[0]], axis=1
                )
            )
        back = dot(jnp.concatenate(rows, axis=0).astype(BF16), table_ref[2])
        columns = []
        for h in range(2):
            re, im = back[h * EDGE : (h + 1) * EDGE, :EDGE], back[h * EDGE : (h + 1) * EDGE, EDGE:]
            columns.append(jnp.concatenate([re * tc - im * ts, im * tc + re * ts], axis=0))
        result = dot(table_ref[3], jnp.concatenate(columns, axis=1).astype(BF16))
        for h in range(2):
            for part in range(2):
                turned_ref[part, pl.ds(b + h, EDGE, stride=ROWS), :] = result[
                    part * EDGE : (part + 1) * EDGE, h * EDGE : (h + 1) * EDGE
                ]
        return carry

    lax.fori_loop(0, ROWS // 4, pair, 0, unroll=UNROLL)
    pl.semaphore_wait(y_sem, 3)
    for i in range(1, 8):
        signal(z_sem, x, y, (z + i) % 8, core)
    lax.fori_loop(ROWS // 4, ROWS // 2, pair, 0, unroll=UNROLL)
    low_half = lax.broadcasted_iota(jnp.int32, (ROWS, EDGE), 1) < EDGE // 2

    def target(t):
        z_step = jnp.where(core == 0, t % 8, (8 - t % 8) % 8)
        x_step = (t // 8 + z_step) % 4
        y_step = (t // 32 + z_step // 2) % 4
        return device_at((x + x_step) % 4, (y + y_step) % 4, (z + z_step) % 8, 0)

    def pack(t, carry):
        to_wide, to_narrow = target(t)
        u = to_wide * 2 + to_narrow // 2
        rows = pl.ds(pl.multiple_of(u * ROWS, ROWS), ROWS)
        re, im = turned_ref[0, rows, :], turned_ref[1, rows, :]
        send_ref[2 * u] = jnp.where(low_half, re, pltpu.roll(im, EDGE // 2, 1)).astype(BF16)
        send_ref[2 * u + 1] = jnp.where(low_half, pltpu.roll(re, EDGE // 2, 1), im).astype(BF16)
        return carry

    def start(to_wide, to_narrow, to):
        pltpu.make_async_remote_copy(
            send_ref.at[to], got_ref.at[me], send_sem, recv_sem,
            device_id={"wide": to_wide, "narrow": to_narrow}, device_id_type=MESH_IDS,
        ).start()

    def spread_out(t, carry):
        to_wide, to_narrow = target(t)
        to = to_wide * 4 + to_narrow
        start(to_wide, to_narrow, to)
        start(to_wide, to_narrow + 1, to + 1)
        return carry

    lax.fori_loop(0, 16, pack, 0, unroll=8)
    pl.semaphore_wait(z_sem, 7)
    start(wide, narrow + 1 - 2 * core, me + 1 - 2 * core)
    lax.fori_loop(1, 16, spread_out, 0)

    def chunk(i, carry):
        def packs(j, inner_carry):
            for n in range(8):
                pack(16 * i + 8 * j + n, 0)
            return inner_carry

        lax.fori_loop(0, 2, packs, 0)
        lax.fori_loop(16 * i, 16 * i + 16, spread_out, 0)
        return carry

    lax.fori_loop(1, EDGE // 16, chunk, 0)
    own = pltpu.make_async_copy(send_ref.at[me], got_ref.at[me], own_sem)
    own.start()
    own.wait()

    for load in loads[3:]:
        load.wait()
    order_curve(angle_ref, curve_ref)
    for i in range(PHASES * TAPS):
        tap = kernel_ref[i // TAPS : i // TAPS + 1, i % TAPS : i % TAPS + 1]
        taps_ref[i] = jnp.broadcast_to(tap, (16, EDGE)).astype(BF16)
    scale_row, scale_column = me // 2 % 8, me % 2 * OWN

    def prepare(r, carry):
        prepare_rows(
            r, scale_ref[scale_row, scale_column + r], rate_ref[scale_row, scale_column + r] * 0.5,
            curve_ref, square_ref, taps_ref, bit_ref, weight_ref, phase_ref,
        )
        return carry

    lax.fori_loop(0, OWN, prepare, 0)
    others = pltpu.make_async_remote_copy(
        send_ref.at[pl.ds(0, DEVICES - 1)], got_ref.at[pl.ds(0, DEVICES - 1)], send_sem, recv_sem,
        device_id={"wide": wide, "narrow": (narrow + 1) % 4}, device_id_type=MESH_IDS,
    )
    others.wait_send()
    others.wait_recv()


    half = EDGE // 2
    split_pairs(got_ref, re_ref, im_ref)
    low_transform(re_ref, im_ref, -1, 8, low_store(re_ref, im_ref))

    def high(k, carry):
        re, im = re_ref[k], im_ref[k]
        left = jnp.concatenate(
            [re, pltpu.roll(re, half, 1), im, pltpu.roll(im, half, 1)], axis=0
        ).astype(BF16)
        result = lax.dot_general(
            left, azimuth_ref[k], (((0,), (0,)), ((), ())), preferred_element_type=F32
        )
        for part in range(2):
            wide_ref[part, pl.ds(k, OWN, stride=LOW), :] = result[:OWN, part * EDGE : (part + 1) * EDGE]
        return carry

    halos = []
    for h in range(2):
        lax.fori_loop(16 * h, 16 * h + 16, high, 0, unroll=4)

        def narrowed(r, carry, h=h):
            rows = pl.ds(pl.multiple_of(r * LOW + 16 * h, 16), 16)
            for part in range(2):
                padded_ref[part, HALO + r, 16 * h : 16 * h + 16, :] = wide_ref[part, rows, :].astype(BF16)
            return carry

        lax.fori_loop(0, OWN, narrowed, 0, unroll=8)
        k_rows = pl.ds(16 * h, 16)
        for side in range(2):
            other = (me + 1 - 2 * side + DEVICES) % DEVICES
            first = OWN if side == 0 else HALO
            target = head_ref if side == 0 else tail_ref
            halo = pltpu.make_async_remote_copy(
                padded_ref.at[:, pl.ds(first, HALO), k_rows, :], target.at[:, :, k_rows, :],
                halo_send.at[2 * h + side], halo_recv.at[2 * h + side],
                device_id={"wide": other // 4, "narrow": other % 4}, device_id_type=MESH_IDS,
            )
            halo.start()
            halos.append(halo)

    def store(r, h, re, im):
        rows = pl.ds(pl.multiple_of(r * LOW + 16 * h, 16), 16)
        turned_ref[0, rows, :] = re
        turned_ref[1, rows, :] = im

    def migrate(r, halves):
        migrate_rows(
            r, scale_ref[scale_row, scale_column + r], halves, padded_ref, bit_ref, weight_ref, phase_ref, store
        )

    def inner(r, carry):
        migrate(r, (0, 1))
        return carry

    lax.fori_loop(HALO, OWN - HALO, inner, 0)

    def finish(h, rows, re, im):
        image_ref[0, rows, h * EDGE : (h + 1) * EDGE] = re.astype(BF16)
        image_ref[1, rows, h * EDGE : (h + 1) * EDGE] = im.astype(BF16)

    def invert(spans, first, stride, begin=None):
        def back(k, carry):
            left = jnp.concatenate(
                [
                    jnp.concatenate(
                        [turned_ref[part, pl.ds(start * LOW + k, count, stride=LOW), :] for start, count in spans], axis=0
                    )
                    for part in range(2)
                ],
                axis=1,
            ).astype(BF16)
            result = dot(left, inverse_ref[k])
            done = 0
            for start, count in spans:
                re_ref[k, start : start + count, :] = result[done : done + count, :EDGE]
                im_ref[k, start : start + count, :] = result[done : done + count, EDGE:]
                done += count
            return carry

        if begin is not None:
            lax.fori_loop(begin, begin + LOW // 2, back, 0, unroll=4)
        else:
            lax.fori_loop(0, LOW, back, 0, unroll=4)
        if begin == 0:
            return []
        low_transform(re_ref, im_ref, 1, 16, finish, first, 2, stride)
        copies = []
        for start, count in spans:
            rows = pl.ds(start, count)
            copies.append(
                pltpu.make_async_copy(
                    image_ref.at[:, rows, :], image_hbm.at[:, rows, :], image_sems.at[start // HALO]
                )
            )
            copies[-1].start()
        return copies

    writes = invert([(HALO, 2 * HALO)], HALO, HALO)
    for h in range(2):
        for halo in halos[2 * h : 2 * h + 2]:
            halo.wait()

        def edge(r, carry, h=h):
            k_rows = pl.ds(16 * h, 16)
            empty = jnp.zeros((16, EDGE), BF16)
            for part in range(2):
                padded_ref[part, r, k_rows, :] = jnp.where(me == 0, empty, head_ref[part, r, k_rows, :])
                padded_ref[part, HALO + OWN + r, k_rows, :] = jnp.where(
                    me == DEVICES - 1, empty, tail_ref[part, r, k_rows, :]
                )
            return carry

        lax.fori_loop(0, HALO, edge, 0, unroll=4)

        def outer(i, carry, h=h):
            for n in range(2):
                migrate(i + n * 3 * HALO, (h,))
            return carry

        lax.fori_loop(0, HALO, outer, 0)
        writes += invert([(0, HALO), (3 * HALO, HALO)], 0, 3 * HALO, 16 * h)
    for write in writes:
        write.wait()


UNROLL = 2
VMEM_BYTES = 63 << 20


def focused_image(*operands):
    big = pltpu.VMEM((2, EDGE * ROWS, EDGE), F32)
    scratch = [pltpu.VMEM(operand.shape, operand.dtype) for operand in operands[:5]]
    scratch += [pltpu.SMEM((8, EDGE), jnp.int32), pltpu.SMEM((8, EDGE), F32)]
    scratch += [pltpu.VMEM(operand.shape, operand.dtype) for operand in operands[7:]]
    scratch += [
        pltpu.VMEM((2, OWN, PULSES), BF16),
        pltpu.VMEM((2, EDGE, EDGE), F32),
        pltpu.VMEM((LOW, EDGE), F32),
        pltpu.VMEM((PHASES * TAPS, 16, EDGE), BF16),
        pltpu.VMEM((OWN, 4, LOW, EDGE), BF16),
        pltpu.VMEM((OWN, TAPS, LOW, EDGE), BF16),
        pltpu.VMEM((2, OWN, LOW, EDGE), F32),
        pltpu.VMEM((DEVICES, ROWS, EDGE), BF16),
        pltpu.VMEM((DEVICES, ROWS, EDGE), BF16),
        big,
        big,
        pltpu.VMEM((LOW, EDGE // 2, EDGE), F32),
        pltpu.VMEM((LOW, EDGE // 2, EDGE), F32),
        pltpu.VMEM((2, 2 * HALO + OWN + 8, LOW, EDGE), BF16),
        pltpu.VMEM((2, HALO, LOW, EDGE), BF16),
        pltpu.VMEM((2, HALO, LOW, EDGE), BF16),
        pltpu.SemaphoreType.DMA((14,)),
        pltpu.SemaphoreType.REGULAR,
        pltpu.SemaphoreType.REGULAR,
        pltpu.SemaphoreType.DMA,
        pltpu.SemaphoreType.DMA,
        pltpu.SemaphoreType.DMA,
        pltpu.SemaphoreType.DMA((4,)),
        pltpu.SemaphoreType.DMA((4,)),
        pltpu.SemaphoreType.DMA((4,)),
    ]
    return pl.pallas_call(
        main_kernel,
        out_shape=jax.ShapeDtypeStruct((2, OWN, PULSES), BF16),
        in_specs=[pl.BlockSpec(memory_space=pl.ANY)] * 11,
        out_specs=pl.BlockSpec(memory_space=pl.ANY),
        scratch_shapes=scratch,
        compiler_params=pltpu.CompilerParams(
            collective_id=0, has_side_effects=True, vmem_limit_bytes=VMEM_BYTES
        ),
        name="focused_image",
    )(*operands)


def shards(echoes, chirp_spectrum, fm_rate, range_scale, doppler_curve, kernels):
    tables, twiddles = range_tables()
    forward, inverse = azimuth_tables()
    index = np.arange(PULSES)
    signed = (index + PULSES // 2) % PULSES - PULSES // 2
    square = np.ascontiguousarray((signed * signed).astype(np.float32).reshape(EDGE, LOW).T)
    return focused_image(
        echoes, chirp_spectrum, jnp.asarray(tables), jnp.asarray(twiddles), jnp.asarray(forward),
        range_scale.reshape(EDGE, EDGE), fm_rate.reshape(EDGE, EDGE),
        doppler_curve.reshape(LOW, EDGE), jnp.asarray(square), kernels, jnp.asarray(inverse),
    )


def solution(mesh):
    in_specs = (P(None, AXES, None), P(), P(), P(), P(), P())
    out_specs = P(None, AXES, None)
    return jax.shard_map(shards, mesh=mesh, in_specs=in_specs, out_specs=out_specs, check_vma=False)
```

```python
import functools
import math

import jax
import jax.numpy as jnp
import ml_dtypes
import numpy as np
from jax import lax
from jax.experimental import pallas as pl
from jax.experimental.pallas import tpu as pltpu
from jax.sharding import PartitionSpec as P

PULSES = 4096
BINS = 16384
EDGE = 128
LOW = 32
TAPS = 8
PHASES = 8
HALO = 16
DEVICES = 256
OWN = BINS // DEVICES
ROWS = PULSES // DEVICES
AXES = ("wide", "narrow")
F32 = jnp.float32
BF16 = jnp.bfloat16


def roots(product, total):
    angles = 2.0 * np.pi / total * (product % total)
    return np.cos(angles), np.sin(angles)


def range_tables():
    count = np.arange(EDGE)
    c, s = roots(np.outer(count, count), EDGE)
    c, s = c / math.sqrt(EDGE), s / math.sqrt(EDGE)
    fwd_left = np.block([[c, s], [-s, c]])
    inv_left = np.block([[c, -s], [s, c]])
    tables = np.stack([fwd_left, fwd_left.T, inv_left.T, inv_left])
    tc, ts = roots(np.outer(count, count), BINS)
    return tables.astype(ml_dtypes.bfloat16), np.stack([tc, ts]).astype(np.float32)


def azimuth_tables():
    low = np.arange(LOW)[:, None, None]
    n = np.arange(EDGE)[None, :, None]
    j = np.arange(EDGE)[None, None, :]
    c, s = roots(n * (low + LOW * j), PULSES)
    forward = np.concatenate(
        [np.concatenate([c, -s], axis=2), np.concatenate([s, c], axis=2)], axis=1
    ) / math.sqrt(PULSES)
    inverse = np.ascontiguousarray(forward.transpose(0, 2, 1))
    return forward.astype(ml_dtypes.bfloat16), inverse.astype(ml_dtypes.bfloat16)


def fft(values, sign):
    count = len(values)
    if count == 1:
        return values
    even, odd = fft(values[0::2], sign), fft(values[1::2], sign)
    half = count // 2
    out = [None] * count
    for k in range(half):
        (ar, ai), (br, bi) = even[k], odd[k]
        if k == 0:
            tr, ti = br, bi
        elif 4 * k == count:
            tr, ti = (-bi, br) if sign > 0 else (bi, -br)
        else:
            angle = 2.0 * math.pi * k / count
            c, s = math.cos(angle), sign * math.sin(angle)
            if 8 * k == count:
                tr, ti = (br - bi * (1 if sign > 0 else -1)) * c, (bi + br * (1 if sign > 0 else -1)) * c
            else:
                tr, ti = br * c - bi * s, br * s + bi * c
        out[k] = (ar + tr, ai + ti)
        out[k + half] = (ar - tr, ai - ti)
    return out


def dot(a, b):
    return jnp.dot(a, b, preferred_element_type=F32)


MESH_IDS = pl.DeviceIdType.MESH


def place():
    wide, narrow = lax.axis_index("wide"), lax.axis_index("narrow")
    return wide % 4, (narrow // 2) * 2 + wide // 32, (wide // 4) % 8, narrow % 2


def device_at(x, y, z, core):
    return ((y % 2) * 8 + z) * 4 + x, (y // 2) * 2 + core


def signal(semaphore, x, y, z, core):
    wide, narrow = device_at(x, y, z, core)
    pl.semaphore_signal(
        semaphore, inc=1, device_id={"wide": wide, "narrow": narrow}, device_id_type=MESH_IDS
    )


def low_transform(re_ref, im_ref, sign, block, store, first=0, count=8, stride=8):
    def step(g, carry):
        rows = pl.ds(pl.multiple_of(first + g * stride, block), block)
        values = fft([(re_ref[m, rows, :], im_ref[m, rows, :]) for m in range(LOW)], sign)
        for k, (re, im) in enumerate(values):
            store(k, rows, re, im)
        return carry

    lax.fori_loop(0, count, step, 0)


def low_store(re_ref, im_ref):
    def store(k, rows, re, im):
        re_ref[k, rows, :] = re
        im_ref[k, rows, :] = im

    return store


def turn(turns):
    x = turns - jnp.round(turns)
    y = x * x
    c = jnp.full_like(x, COS_TERMS[-1])
    for term in COS_TERMS[-2::-1]:
        c = c * y + term
    s = jnp.full_like(x, SIN_TERMS[-1])
    for term in SIN_TERMS[-2::-1]:
        s = s * y + term
    return c, s * x


def fitted_terms():
    x = np.cos(np.pi * (np.arange(400) + 0.5) / 800) * 0.5
    y = x * x
    powers = np.stack([y**i for i in range(6)], axis=1)
    c = np.linalg.lstsq(powers, np.cos(2 * np.pi * x), rcond=None)[0]
    s = np.linalg.lstsq(powers * x[:, None], np.sin(2 * np.pi * x), rcond=None)[0]
    return [float(v) for v in c], [float(v) for v in s]


COS_TERMS, SIN_TERMS = fitted_terms()


def order_curve(angle_ref, curve_ref):
    values = angle_ref[...].astype(F32)
    upper = jnp.floor(values * (1.0 / 64.0))
    lower = values - 64.0 * upper
    row = lax.broadcasted_iota(jnp.int32, (LOW, EDGE), 0)
    lane = lax.broadcasted_iota(jnp.int32, (LOW, EDGE), 1)
    total = jnp.zeros((LOW, EDGE), F32)
    for digit, size in ((upper, 64.0), (lower, 1.0)):
        digit = digit.astype(BF16)
        for i in range(EDGE // LOW):
            pick = jnp.where(lane == LOW * i + row, 1.0, 0.0).astype(BF16)
            part = lax.dot_general(pick, digit, (((1,), (1,)), ((), ())), preferred_element_type=F32)
            place_at = jnp.where(lane == 4 * row + i, 1.0, 0.0).astype(BF16)
            total = total + size * dot(part.astype(BF16), place_at)
    curve_ref[...] = total


def prepare_rows(r, scale, rate, curve_ref, square_ref, taps_ref, bit_ref, weight_ref, phase_ref):
    offset = jnp.where(scale < 0, 8.0 * SHIFT_LOW, 0.0).astype(F32)
    scale = scale.astype(F32) * (1.0 / 4096.0)
    for h in range(2):
        rows = pl.ds(16 * h, 16)
        level = (jnp.floor(curve_ref[rows, :] * scale) + offset).astype(BF16)
        bits = []
        for i, weight in enumerate((64, 32, 16, 8, 4, 2, 1)):
            bit = level >= jnp.asarray(weight, BF16)
            bits.append(bit)
            if i < 4:
                bit_ref[r, i, rows, :] = jnp.where(bit, jnp.asarray(1, BF16), jnp.asarray(0, BF16))
            if weight > 1:
                level = jnp.where(bit, level - jnp.asarray(weight, BF16), level)
        for t in range(TAPS):
            level4 = [jnp.where(bits[6], taps_ref[(2 * i + 1) * TAPS + t], taps_ref[2 * i * TAPS + t]) for i in range(4)]
            level2 = [jnp.where(bits[5], level4[2 * i + 1], level4[2 * i]) for i in range(2)]
            weight_ref[r, t, rows, :] = jnp.where(bits[4], level2[1], level2[0])
        c, s = turn(square_ref[rows, :] * rate)
        phase_ref[0, r, rows, :] = c
        phase_ref[1, r, rows, :] = s


def migrate_rows(r, scale, halves, padded_ref, bit_ref, weight_ref, phase_ref, store):
    first = r + HALO - 3 - jnp.where(scale < 0, SHIFT_LOW, 0)
    for h in halves:
        rows = pl.ds(16 * h, 16)
        bits = [bit_ref[r, i, rows, :] > jnp.asarray(0, BF16) for i in range(4)]
        sums = []
        for part in range(2):
            x = [padded_ref[part, first + i, rows, :] for i in range(21)]
            x = [jnp.where(bits[0], x[i + 8], x[i]) if i < 13 else x[i] for i in range(15)]
            x = [jnp.where(bits[1], x[i + 4], x[i]) for i in range(11)]
            x = [jnp.where(bits[2], x[i + 2], x[i]) for i in range(9)]
            x = [jnp.where(bits[3], x[i + 1], x[i]) for i in range(8)]
            terms = [x[t] * weight_ref[r, t, rows, :] for t in range(TAPS)]
            while len(terms) > 1:
                terms = [terms[i] + terms[i + 1] for i in range(0, len(terms), 2)]
            sums.append(terms[0].astype(F32))
        c, s = phase_ref[0, r, rows, :], phase_ref[1, r, rows, :]
        store(r, h, sums[0] * c - sums[1] * s, sums[0] * s + sums[1] * c)


SHIFT_LOW = 13


def main_kernel(
    echo_hbm, chirp_hbm, table_hbm, twiddle_hbm, azimuth_hbm, scale_hbm, rate_hbm, angle_hbm, square_hbm, kernel_hbm, inverse_hbm,
    image_hbm,
    echo_ref, line_ref, table_ref, twiddle_ref, azimuth_ref, scale_ref, rate_ref, angle_ref, square_ref, kernel_ref, inverse_ref,
    image_ref,
    chirp_ref, curve_ref, taps_ref, bit_ref, weight_ref, phase_ref,
    send_ref, got_ref, wide_ref, turned_ref, re_ref, im_ref, padded_ref, head_ref, tail_ref,
    load_sems, y_sem, z_sem, send_sem, recv_sem, own_sem, halo_send, halo_recv, image_sems,
):
    x, y, z, core = place()
    wide, narrow = device_at(x, y, z, core)
    me = wide * 4 + narrow

    pieces = 4
    echo_loads = []
    for i in range(pieces):
        columns = pl.ds(i * (BINS // pieces), BINS // pieces)
        load = pltpu.make_async_copy(
            echo_hbm.at[:, :, columns], echo_ref.at[:, :, columns], load_sems.at[i]
        )
        load.start()
        echo_loads.append(load)
    own_rows = pl.ds(pl.multiple_of(me // 16 * 8, 8), 8)
    loads = []
    for i, (source, target) in enumerate(
        (
            (chirp_hbm, line_ref), (table_hbm, table_ref), (twiddle_hbm, twiddle_ref),
            (angle_hbm, angle_ref), (square_hbm, square_ref), (kernel_hbm, kernel_ref),
            (scale_hbm.at[own_rows], scale_ref), (rate_hbm.at[own_rows], rate_ref),
            (azimuth_hbm, azimuth_ref), (inverse_hbm, inverse_ref),
        )
    ):
        load = pltpu.make_async_copy(source, target, load_sems.at[pieces + i])
        if i < 8:
            load.start()
        loads.append(load)

    barrier = pltpu.get_barrier_semaphore()
    for i in range(1, 8):
        signal(barrier, (x + i // 2) % 4, y, z, (core + i) % 2)
    for i in range(1, 4):
        signal(barrier, x, (y + i) % 4, z, core)
    for i in range(1, 8):
        signal(barrier, x, y, (z + i) % 8, core)

    def spread(m, carry):
        columns = pl.ds(pl.multiple_of(m * EDGE, EDGE), EDGE)
        for part in range(2):
            block = echo_ref[part, :, columns].astype(F32)
            wide_ref[part, pl.ds(pl.multiple_of(m * ROWS, ROWS), ROWS), :] = block
        return carry

    for i in range(pieces):
        echo_loads[i].wait()
        lax.fori_loop(i * (EDGE // pieces), (i + 1) * (EDGE // pieces), spread, 0, unroll=8)
    for load in loads[:3]:
        load.wait()
    for load in loads[8:]:
        load.start()

    def lay(j, carry):
        for part in range(2):
            chirp_ref[part, pl.ds(j, 1), :] = line_ref[part : part + 1, pl.ds(pl.multiple_of(j * EDGE, EDGE), EDGE)]
        return carry

    lax.fori_loop(0, EDGE, lay, 0, unroll=8)
    for part in range(2):
        chirp_ref[part] = chirp_ref[part].T

    pl.semaphore_wait(barrier, 17)
    for i in range(1, 4):
        signal(y_sem, x, (y + i) % 4, z, core)
    tc, ts = twiddle_ref[0], twiddle_ref[1]

    def pair(i, carry):
        b = 2 * i
        signals = jnp.concatenate(
            [
                jnp.concatenate(
                    [wide_ref[part, pl.ds(b + h, EDGE, stride=ROWS), :] for h in range(2)], axis=1
                )
                for part in range(2)
            ],
            axis=0,
        ).astype(BF16)
        first = dot(table_ref[0], signals)
        rows = []
        for h in range(2):
            re, im = first[:EDGE, h * EDGE : (h + 1) * EDGE], first[EDGE:, h * EDGE : (h + 1) * EDGE]
            rows.append(jnp.concatenate([re * tc + im * ts, im * tc - re * ts], axis=1))
        spectrum = dot(jnp.concatenate(rows, axis=0).astype(BF16), table_ref[1])
        rows = []
        for h in range(2):
            re, im = spectrum[h * EDGE : (h + 1) * EDGE, :EDGE], spectrum[h * EDGE : (h + 1) * EDGE, EDGE:]
            rows.append(
                jnp.concatenate(
                    [re * chirp_ref[0] - im * chirp_ref[1], re * chirp_ref[1] + im * chirp_ref[0]], axis=1
                )
            )
        back = dot(jnp.concatenate(rows, axis=0).astype(BF16), table_ref[2])
        columns = []
        for h in range(2):
            re, im = back[h * EDGE : (h + 1) * EDGE, :EDGE], back[h * EDGE : (h + 1) * EDGE, EDGE:]
            columns.append(jnp.concatenate([re * tc - im * ts, im * tc + re * ts], axis=0))
        result = dot(table_ref[3], jnp.concatenate(columns, axis=1).astype(BF16))
        for h in range(2):
            for part in range(2):
                turned_ref[part, pl.ds(b + h, EDGE, stride=ROWS), :] = result[
                    part * EDGE : (part + 1) * EDGE, h * EDGE : (h + 1) * EDGE
                ]
        return carry

    lax.fori_loop(0, ROWS // 4, pair, 0, unroll=UNROLL)
    pl.semaphore_wait(y_sem, 3)
    for i in range(1, 8):
        signal(z_sem, x, y, (z + i) % 8, core)
    lax.fori_loop(ROWS // 4, ROWS // 2, pair, 0, unroll=UNROLL)
    low_half = lax.broadcasted_iota(jnp.int32, (ROWS, EDGE), 1) < EDGE // 2

    def target(t):
        z_step = jnp.where(core == 0, t % 8, (8 - t % 8) % 8)
        x_step = (t // 8 + z_step) % 4
        y_step = (t // 32 + z_step // 2) % 4
        return device_at((x + x_step) % 4, (y + y_step) % 4, (z + z_step) % 8, 0)

    def pack(t, carry):
        to_wide, to_narrow = target(t)
        u = to_wide * 2 + to_narrow // 2
        rows = pl.ds(pl.multiple_of(u * ROWS, ROWS), ROWS)
        re, im = turned_ref[0, rows, :], turned_ref[1, rows, :]
        send_ref[2 * u] = jnp.where(low_half, re, pltpu.roll(im, EDGE // 2, 1)).astype(BF16)
        send_ref[2 * u + 1] = jnp.where(low_half, pltpu.roll(re, EDGE // 2, 1), im).astype(BF16)
        return carry

    def start(to_wide, to_narrow, to, group):
        pltpu.make_async_remote_copy(
            send_ref.at[to], got_ref.at[me], send_sem, recv_sem.at[group],
            device_id={"wide": to_wide, "narrow": to_narrow}, device_id_type=MESH_IDS,
        ).start()

    def spread_out(t, carry):
        to_wide, to_narrow = target(t)
        to = to_wide * 4 + to_narrow
        start(to_wide, to_narrow, to, t // 16)
        start(to_wide, to_narrow + 1, to + 1, t // 16)
        return carry

    lax.fori_loop(0, 16, pack, 0, unroll=8)
    pl.semaphore_wait(z_sem, 7)
    start(wide, narrow + 1 - 2 * core, me + 1 - 2 * core, 0)
    lax.fori_loop(1, 16, spread_out, 0)

    def chunk(i, carry):
        def packs(j, inner_carry):
            for n in range(8):
                pack(16 * i + 8 * j + n, 0)
            return inner_carry

        lax.fori_loop(0, 2, packs, 0)
        lax.fori_loop(16 * i, 16 * i + 16, spread_out, 0)
        return carry

    lax.fori_loop(1, EDGE // 16, chunk, 0)
    own = pltpu.make_async_copy(send_ref.at[me], got_ref.at[me], own_sem)
    own.start()
    own.wait()

    for load in loads[3:]:
        load.wait()
    order_curve(angle_ref, curve_ref)
    for i in range(PHASES * TAPS):
        tap = kernel_ref[i // TAPS : i // TAPS + 1, i % TAPS : i % TAPS + 1]
        taps_ref[i] = jnp.broadcast_to(tap, (16, EDGE)).astype(BF16)
    scale_row, scale_column = me // 2 % 8, me % 2 * OWN

    def prepare(r, carry):
        prepare_rows(
            r, scale_ref[scale_row, scale_column + r], rate_ref[scale_row, scale_column + r] * 0.5,
            curve_ref, square_ref, taps_ref, bit_ref, weight_ref, phase_ref,
        )
        return carry

    lax.fori_loop(0, OWN, prepare, 0)
    half = EDGE // 2
    upper_half = lax.broadcasted_iota(jnp.int32, (ROWS, EDGE), 1) // half

    def messages(first, count, semaphore):
        return pltpu.make_async_remote_copy(
            send_ref.at[pl.ds(first, count)], got_ref.at[pl.ds(first, count)], send_sem, semaphore,
            device_id={"wide": wide, "narrow": (narrow + 1) % 4}, device_id_type=MESH_IDS,
        )

    def take(t, from_core):
        z_step = t % 8 if from_core == 0 else (8 - t % 8) % 8
        x_step = (t // 8 + z_step) % 4
        y_step = (t // 32 + z_step // 2) % 4
        from_x = (x - x_step + 4) % 4
        from_wide, from_narrow = device_at(from_x, (y - y_step + 4) % 4, (z - z_step + 8) % 8, from_core)
        odd = from_x % 2
        message = got_ref[from_wide * 4 + from_narrow].astype(F32)
        turned = pltpu.roll(message, half, 1)
        m = from_wide // 2
        rows = pl.ds(pl.multiple_of(from_narrow * ROWS, ROWS), ROWS)
        kept = upper_half == odd
        re_ref[m, rows, :] = jnp.where(kept, jnp.where(odd == 0, message, turned), re_ref[m, rows, :])
        im_ref[m, rows, :] = jnp.where(kept, jnp.where(odd == 0, turned, message), im_ref[m, rows, :])

    def takes(t, carry):
        take(t, 0)
        take(t, 1)
        return carry

    messages(0, 31, recv_sem.at[0]).wait_recv()
    lax.fori_loop(0, 16, takes, 0, unroll=2)

    def group(i, carry):
        messages(0, 32, recv_sem.at[i]).wait_recv()

        def two(j, inner_carry):
            takes(16 * i + 2 * j, 0)
            takes(16 * i + 2 * j + 1, 0)
            return inner_carry

        lax.fori_loop(0, 8, two, 0)
        return carry

    lax.fori_loop(1, 8, group, 0)
    messages(0, DEVICES - 1, recv_sem.at[0]).wait_send()

    low_transform(re_ref, im_ref, -1, 8, low_store(re_ref, im_ref))

    def high(k, carry):
        re, im = re_ref[k], im_ref[k]
        left = jnp.concatenate(
            [re, pltpu.roll(re, half, 1), im, pltpu.roll(im, half, 1)], axis=0
        ).astype(BF16)
        result = lax.dot_general(
            left, azimuth_ref[k], (((0,), (0,)), ((), ())), preferred_element_type=F32
        )
        for part in range(2):
            wide_ref[part, pl.ds(k, OWN, stride=LOW), :] = result[:OWN, part * EDGE : (part + 1) * EDGE]
        return carry

    halos = []
    for h in range(2):
        lax.fori_loop(16 * h, 16 * h + 16, high, 0, unroll=4)

        def narrowed(r, carry, h=h):
            rows = pl.ds(pl.multiple_of(r * LOW + 16 * h, 16), 16)
            for part in range(2):
                padded_ref[part, HALO + r, 16 * h : 16 * h + 16, :] = wide_ref[part, rows, :].astype(BF16)
            return carry

        lax.fori_loop(0, OWN, narrowed, 0, unroll=8)
        k_rows = pl.ds(16 * h, 16)
        for side in range(2):
            other = (me + 1 - 2 * side + DEVICES) % DEVICES
            first = OWN if side == 0 else HALO
            target = head_ref if side == 0 else tail_ref
            halo = pltpu.make_async_remote_copy(
                padded_ref.at[:, pl.ds(first, HALO), k_rows, :], target.at[:, :, k_rows, :],
                halo_send.at[2 * h + side], halo_recv.at[2 * h + side],
                device_id={"wide": other // 4, "narrow": other % 4}, device_id_type=MESH_IDS,
            )
            halo.start()
            halos.append(halo)

    def store(r, h, re, im):
        rows = pl.ds(pl.multiple_of(r * LOW + 16 * h, 16), 16)
        turned_ref[0, rows, :] = re
        turned_ref[1, rows, :] = im

    def migrate(r, halves):
        migrate_rows(
            r, scale_ref[scale_row, scale_column + r], halves, padded_ref, bit_ref, weight_ref, phase_ref, store
        )

    def inner(r, carry):
        migrate(r, (0, 1))
        return carry

    lax.fori_loop(HALO, OWN - HALO, inner, 0)

    def finish(h, rows, re, im):
        image_ref[0, rows, h * EDGE : (h + 1) * EDGE] = re.astype(BF16)
        image_ref[1, rows, h * EDGE : (h + 1) * EDGE] = im.astype(BF16)

    def invert(spans, first, stride, begin=None):
        def back(k, carry):
            left = jnp.concatenate(
                [
                    jnp.concatenate(
                        [turned_ref[part, pl.ds(start * LOW + k, count, stride=LOW), :] for start, count in spans], axis=0
                    )
                    for part in range(2)
                ],
                axis=1,
            ).astype(BF16)
            result = dot(left, inverse_ref[k])
            done = 0
            for start, count in spans:
                re_ref[k, start : start + count, :] = result[done : done + count, :EDGE]
                im_ref[k, start : start + count, :] = result[done : done + count, EDGE:]
                done += count
            return carry

        if begin is not None:
            lax.fori_loop(begin, begin + LOW // 2, back, 0, unroll=4)
        else:
            lax.fori_loop(0, LOW, back, 0, unroll=4)
        if begin == 0:
            return []
        low_transform(re_ref, im_ref, 1, 16, finish, first, 2, stride)
        copies = []
        for start, count in spans:
            rows = pl.ds(start, count)
            copies.append(
                pltpu.make_async_copy(
                    image_ref.at[:, rows, :], image_hbm.at[:, rows, :], image_sems.at[start // HALO]
                )
            )
            copies[-1].start()
        return copies

    writes = invert([(HALO, 2 * HALO)], HALO, HALO)
    for h in range(2):
        for halo in halos[2 * h : 2 * h + 2]:
            halo.wait()

        def edge(r, carry, h=h):
            k_rows = pl.ds(16 * h, 16)
            empty = jnp.zeros((16, EDGE), BF16)
            for part in range(2):
                padded_ref[part, r, k_rows, :] = jnp.where(me == 0, empty, head_ref[part, r, k_rows, :])
                padded_ref[part, HALO + OWN + r, k_rows, :] = jnp.where(
                    me == DEVICES - 1, empty, tail_ref[part, r, k_rows, :]
                )
            return carry

        lax.fori_loop(0, HALO, edge, 0, unroll=4)

        def outer(i, carry, h=h):
            for n in range(2):
                migrate(i + n * 3 * HALO, (h,))
            return carry

        lax.fori_loop(0, HALO, outer, 0)
        writes += invert([(0, HALO), (3 * HALO, HALO)], 0, 3 * HALO, 16 * h)
    for write in writes:
        write.wait()


UNROLL = 2
VMEM_BYTES = 63 << 20


def focused_image(*operands):
    big = pltpu.VMEM((2, EDGE * ROWS, EDGE), F32)
    scratch = [pltpu.VMEM(operand.shape, operand.dtype) for operand in operands[:5]]
    scratch += [pltpu.SMEM((8, EDGE), jnp.int32), pltpu.SMEM((8, EDGE), F32)]
    scratch += [pltpu.VMEM(operand.shape, operand.dtype) for operand in operands[7:]]
    scratch += [
        pltpu.VMEM((2, OWN, PULSES), BF16),
        pltpu.VMEM((2, EDGE, EDGE), F32),
        pltpu.VMEM((LOW, EDGE), F32),
        pltpu.VMEM((PHASES * TAPS, 16, EDGE), BF16),
        pltpu.VMEM((OWN, 4, LOW, EDGE), BF16),
        pltpu.VMEM((OWN, TAPS, LOW, EDGE), BF16),
        pltpu.VMEM((2, OWN, LOW, EDGE), F32),
        pltpu.VMEM((DEVICES, ROWS, EDGE), BF16),
        pltpu.VMEM((DEVICES, ROWS, EDGE), BF16),
        big,
        big,
        pltpu.VMEM((LOW, EDGE // 2, EDGE), F32),
        pltpu.VMEM((LOW, EDGE // 2, EDGE), F32),
        pltpu.VMEM((2, 2 * HALO + OWN + 8, LOW, EDGE), BF16),
        pltpu.VMEM((2, HALO, LOW, EDGE), BF16),
        pltpu.VMEM((2, HALO, LOW, EDGE), BF16),
        pltpu.SemaphoreType.DMA((14,)),
        pltpu.SemaphoreType.REGULAR,
        pltpu.SemaphoreType.REGULAR,
        pltpu.SemaphoreType.DMA,
        pltpu.SemaphoreType.DMA((8,)),
        pltpu.SemaphoreType.DMA,
        pltpu.SemaphoreType.DMA((4,)),
        pltpu.SemaphoreType.DMA((4,)),
        pltpu.SemaphoreType.DMA((4,)),
    ]
    return pl.pallas_call(
        main_kernel,
        out_shape=jax.ShapeDtypeStruct((2, OWN, PULSES), BF16),
        in_specs=[pl.BlockSpec(memory_space=pl.ANY)] * 11,
        out_specs=pl.BlockSpec(memory_space=pl.ANY),
        scratch_shapes=scratch,
        compiler_params=pltpu.CompilerParams(
            collective_id=0, has_side_effects=True, vmem_limit_bytes=VMEM_BYTES
        ),
        name="focused_image",
    )(*operands)


def shards(echoes, chirp_spectrum, fm_rate, range_scale, doppler_curve, kernels):
    tables, twiddles = range_tables()
    forward, inverse = azimuth_tables()
    index = np.arange(PULSES)
    signed = (index + PULSES // 2) % PULSES - PULSES // 2
    square = np.ascontiguousarray((signed * signed).astype(np.float32).reshape(EDGE, LOW).T)
    return focused_image(
        echoes, chirp_spectrum, jnp.asarray(tables), jnp.asarray(twiddles), jnp.asarray(forward),
        range_scale.reshape(EDGE, EDGE), fm_rate.reshape(EDGE, EDGE),
        doppler_curve.reshape(LOW, EDGE), jnp.asarray(square), kernels, jnp.asarray(inverse),
    )


def solution(mesh):
    in_specs = (P(None, AXES, None), P(), P(), P(), P(), P())
    out_specs = P(None, AXES, None)
    return jax.shard_map(shards, mesh=mesh, in_specs=in_specs, out_specs=out_specs, check_vma=False)
```
